32 devices in a mesh: section: 2 (over x), dp: 16 (over z, y, core).
Axes of the slice: x: 2, y: 2, z: 4, core: 2. Of those that a mesh axis runs over, the one named last changes fastest.
Arguments:
- tokens: bfloat16 [16384, 384], P('dp'), may hold values from -6 to 6
- cotangent: float32 [16384, 384], P('dp'), may hold values from -6 to 6
- seq_lengths: int32 [32, 4], P('dp'), may hold values from 0 to 512, as said below
- query_weight: bfloat16 [2, 384, 384], P('section'), may hold values from -0.3125 to 0.3125
- query_bias: bfloat16 [2, 384], P('section'), may hold values from -4 to 4
- key_weight: bfloat16 [2, 384, 384], P('section'), may hold values from -0.3125 to 0.3125
- key_bias: bfloat16 [2, 384], P('section'), may hold values from -4 to 4
- value_weight: bfloat16 [2, 384, 384], P('section'), may hold values from -0.3125 to 0.3125
- value_bias: bfloat16 [2, 384], P('section'), may hold values from -1.5 to 1.5
- output_weight: bfloat16 [2, 384, 384], P('section'), may hold values from -1.25 to 1.25
- output_bias: bfloat16 [2, 384], P('section'), may hold values from -6 to 6
- first_gain: bfloat16 [2, 384], P('section'), may hold values from 0.25 to 1.75
- first_shift: bfloat16 [2, 384], P('section'), may hold values from -6 to 6
- inner_weight: bfloat16 [2, 384, 1536], P('section'), may hold values from -0.3125 to 0.3125
- inner_bias: bfloat16 [2, 1536], P('section'), may hold values from -6 to 6
- outer_weight: bfloat16 [2, 1536, 384], P('section'), may hold values from -0.15625 to 0.15625
- outer_bias: bfloat16 [2, 384], P('section'), may hold values from -6 to 6
- second_gain: bfloat16 [2, 384], P('section'), may hold values from 0.25 to 1.75
- second_shift: bfloat16 [2, 384], P('section'), may hold values from -6 to 6
Outputs:
- layer_outputs: bfloat16 [2, 16384, 384], P('section', 'dp')
- input_grads: float32 [2, 16384, 384], P('section', 'dp')
- query_weight_gradient: float32 [2, 384, 384], P('section')
- query_bias_gradient: float32 [2, 384], P('section')
- key_weight_gradient: float32 [2, 384, 384], P('section')
- key_bias_gradient: float32 [2, 384], P('section')
- value_weight_gradient: float32 [2, 384, 384], P('section')
- value_bias_gradient: float32 [2, 384], P('section')
- output_weight_gradient: float32 [2, 384, 384], P('section')
- output_bias_gradient: float32 [2, 384], P('section')
- first_gain_gradient: float32 [2, 384], P('section')
- first_shift_gradient: float32 [2, 384], P('section')
- inner_weight_gradient: float32 [2, 384, 1536], P('section')
- inner_bias_gradient: float32 [2, 1536], P('section')
- outer_weight_gradient: float32 [2, 1536, 384], P('section')
- outer_bias_gradient: float32 [2, 384], P('section')
- second_gain_gradient: float32 [2, 384], P('section')
- second_shift_gradient: float32 [2, 384], P('section')
The draws below stay inside these ranges and needn't reach their ends.
Inputs may be any that keep to these rules, and one draw needn't show every extreme that they name: `seq_lengths`: each row gives the lengths of up to 4 sequences packed from the start of one block of 512 places (a length may be 0); a row's lengths add up to at most 512, and in every draw one row holds a single sequence of 512.
All inputs are finite; a program needn't handle non-finite values.
Results may differ from the reference program's by a relative error of at most 0.03.
Values may be sent and summed in bfloat16 or wider, within the bound.
No kernel may reach another device: no remote copies, remote signals or barrier semaphores. Data moves between devices by JAX's collectives and lax.ppermute only.
A program may use at most 192 MiB of HBM per device.

```python
import math
import jax
import jax.numpy as jnp
from jax import lax

D = 384
HEADS = 6
HEAD_DIM = 64
FF = 1536
SEQ_LEN = 512
SEQS = 4
TOKENS = 16384
N_SECTION = 2


def draw_seq_lengths(key, part):
    key = jax.random.fold_in(key, 7)
    row_count = TOKENS // SEQ_LEN
    level_key, cut_key, full_key = jax.random.split(key, 3)
    levels = jax.random.randint(level_key, (row_count,), 0, 8)
    halvings = jnp.where(levels < 4, 0, jnp.where(levels < 6, 1, jnp.where(levels < 7, 2, 3))).astype(jnp.int32)
    used_places = jnp.right_shift(jnp.full((row_count,), SEQ_LEN, jnp.int32), halvings)
    cut_points = jax.random.randint(cut_key, (row_count, SEQS - 1), 0, 1 << 20) % (used_places[:, None] + 1)
    bounds = jnp.concatenate([jnp.zeros((row_count, 1), jnp.int32), cut_points.astype(jnp.int32), used_places[:, None]], axis=1)
    bounds = jnp.sort(bounds, axis=1)
    lengths_out = bounds[:, 1:] - bounds[:, :-1]
    chosen = jax.random.randint(full_key, (), 0, row_count)
    single = jnp.zeros((SEQS,), jnp.int32).at[0].set(SEQ_LEN)
    lengths_out = jnp.where((jnp.arange(row_count) == chosen)[:, None], single[None, :], lengths_out)
    return lengths_out.astype(jnp.int32)


def steps_of(stream_key, dims, shards, least, high):
    level = 1.0
    for dim, parts in shards:
        draws = jax.random.uniform(jax.random.fold_in(jax.random.fold_in(stream_key, 6), dim), (parts,), jnp.float32, least / len(shards), high / len(shards))
        level = level * jnp.repeat(jnp.exp(draws), dims[dim] // parts).reshape((-1,) + (1,) * (len(dims) - 1 - dim))
    return level


def bell_draw(key, dims, scale, bound, cuts=(), kind=jnp.bfloat16):
    factor_of = steps_of(key, dims, cuts, -0.22, 0.18) if cuts else 1.0
    values = jax.random.normal(key, dims, jnp.float32) * scale * factor_of
    return jnp.minimum(jnp.maximum(values, -bound), bound).astype(kind)


def setup_inputs(seed: int = 0) -> dict:
    splits = jax.random.split(jax.random.key(seed), 20)
    return {
        "tokens": bell_draw(splits[0], (TOKENS, D), 1.0, 6.0, ((0, 16),)),
        "cotangent": bell_draw(splits[1], (TOKENS, D), 1.0, 6.0, ((0, 16),), jnp.float32),
        "seq_lengths": draw_seq_lengths(jax.random.fold_in(splits[19], 71), 0),
        "query_weight": bell_draw(splits[3], (N_SECTION, D, D), D ** -0.5, 0.3125, ((0, 2),)),
        "query_bias": bell_draw(splits[4], (N_SECTION, D), 0.3, 4.0, ((0, 2),)),
        "key_weight": bell_draw(splits[5], (N_SECTION, D, D), D ** -0.5, 0.3125, ((0, 2),)),
        "key_bias": bell_draw(splits[6], (N_SECTION, D), 0.3, 4.0, ((0, 2),)),
        "value_weight": bell_draw(splits[7], (N_SECTION, D, D), D ** -0.5, 0.3125, ((0, 2),)),
        "value_bias": bell_draw(splits[8], (N_SECTION, D), 0.1, 1.5, ((0, 2),)),
        "output_weight": bell_draw(splits[9], (N_SECTION, D, D), (D // 16) ** -0.5, 1.25, ((0, 2),)),
        "output_bias": bell_draw(splits[10], (N_SECTION, D), 0.5, 6.0, ((0, 2),)),
        "first_gain": jnp.clip(1.0 + 0.15 * jax.random.normal(splits[11], (N_SECTION, D), jnp.float32), 0.25, 1.75).astype(jnp.bfloat16),
        "first_shift": bell_draw(splits[12], (N_SECTION, D), 0.5, 6.0, ((0, 2),)),
        "inner_weight": bell_draw(splits[13], (N_SECTION, D, FF), D ** -0.5, 0.3125, ((0, 2),)),
        "inner_bias": bell_draw(splits[14], (N_SECTION, FF), 0.5, 6.0, ((0, 2),)),
        "outer_weight": bell_draw(splits[15], (N_SECTION, FF, D), FF ** -0.5, 0.15625, ((0, 2),)),
        "outer_bias": bell_draw(splits[16], (N_SECTION, D), 0.5, 6.0, ((0, 2),)),
        "second_gain": jnp.clip(1.0 + 0.15 * jax.random.normal(splits[17], (N_SECTION, D), jnp.float32), 0.25, 1.75).astype(jnp.bfloat16),
        "second_shift": bell_draw(splits[18], (N_SECTION, D), 0.5, 6.0, ((0, 2),)),
    }


@jax.custom_vjp
def low(v):
    return lax.optimization_barrier(v.astype(jnp.bfloat16)).astype(jnp.float32)

@jax.custom_vjp
def low_back(v):
    return v

def low_keep(v):
    return (low(v), None)

def low_pass(kept, grad):
    return (grad,)

def back_keep(v):
    return (v, None)

def back_low(kept, grad):
    return (low(grad),)
low.defvjp(low_keep, low_pass)
low_back.defvjp(back_keep, back_low)
norm_eps = 1e-12
rope_base = 10000.0
mask_fill = -1000000000.0

def rotary_tables(lengths_row, length, model_width, head_size):
    places = jnp.arange(length, dtype=jnp.int32)
    seq_ends = jnp.cumsum(lengths_row).astype(jnp.int32)
    passed = (places[:, None] >= seq_ends[None, :]).astype(jnp.int32)
    segment = lax.optimization_barrier(jnp.sum(passed, axis=1)).astype(jnp.int32)
    offset = lax.optimization_barrier(jnp.sum(passed * lengths_row[None, :], axis=1)).astype(jnp.int32)
    position = (places - offset).astype(jnp.float32)
    live_rows = (places < seq_ends[-1]).astype(jnp.float32)
    pair_index = (jnp.arange(model_width // 2, dtype=jnp.int32) % (head_size // 2)).astype(jnp.float32)
    inverse = jnp.exp(pair_index * (-2.0 * math.log(rope_base) / head_size))
    angles = position[:, None] * inverse[None, :]
    return (segment, live_rows, jnp.cos(angles), jnp.sin(angles))

def rotate(values, cosine_table, sine_table):
    even_part = values[:, 0::2]
    odd_part = values[:, 1::2]
    first_part = even_part * cosine_table - odd_part * sine_table
    second_part = odd_part * cosine_table + even_part * sine_table
    return jnp.stack([first_part, second_part], axis=-1).reshape(values.shape)

def normalize(summed):
    centered = summed - lax.optimization_barrier(jnp.mean(summed, axis=-1, keepdims=True))
    inverse_std = lax.rsqrt(lax.optimization_barrier(jnp.mean(centered * centered, axis=-1, keepdims=True)) + norm_eps)
    return centered * inverse_std

def product(left, right):
    return jnp.dot(left, right, precision=lax.Precision.HIGHEST)

def layer_forward(inputs, weights, lengths_row):
    query_weight, query_bias, key_weight, key_bias, value_weight, value_bias, output_weight, output_bias, first_gain, first_shift, inner_weight, inner_bias, outer_weight, outer_bias, second_gain, second_shift = weights
    segment, live_rows, cosine_table, sine_table = rotary_tables(lengths_row, SEQ_LEN, D, HEAD_DIM)
    query_pre = low_back(product(inputs, query_weight) + query_bias)
    key_pre = low_back(product(inputs, key_weight) + key_bias)
    queries = low(rotate(query_pre, cosine_table, sine_table)).reshape(SEQ_LEN, HEADS, HEAD_DIM)
    keys_rot = low(rotate(key_pre, cosine_table, sine_table)).reshape(SEQ_LEN, HEADS, HEAD_DIM)
    values_low = low(low_back(product(inputs, value_weight) + value_bias)).reshape(SEQ_LEN, HEADS, HEAD_DIM)
    scores = jnp.einsum('qhd,khd->hqk', queries, keys_rot, precision=lax.Precision.HIGHEST)
    scores = low_back(scores * HEAD_DIM ** (-0.5))
    allowed = segment[:, None] == segment[None, :]
    scores = jnp.where(allowed[None], scores, mask_fill)
    shares = low(jax.nn.softmax(scores, axis=-1))
    context = jnp.einsum('hqk,khd->qhd', shares, values_low, precision=lax.Precision.HIGHEST)
    context = low(low_back(context.reshape(SEQ_LEN, D)))
    attended = low_back(product(context, output_weight) + output_bias)
    first_out = normalize(inputs + attended) * first_gain + first_shift
    inner = low_back(product(low(first_out), inner_weight) + inner_bias)
    hidden = low(jax.nn.gelu(inner, approximate=False))
    outer = low_back(product(hidden, outer_weight) + outer_bias)
    second_out = normalize(first_out + outer) * second_gain + second_shift
    return second_out * live_rows[:, None]

def reference(tokens, cotangent, seq_lengths, query_weight, query_bias, key_weight, key_bias, value_weight, value_bias, output_weight, output_bias, first_gain, first_shift, inner_weight, inner_bias, outer_weight, outer_bias, second_gain, second_shift):
    params = tuple((member.astype(jnp.float32) for member in (query_weight, query_bias, key_weight, key_bias, value_weight, value_bias, output_weight, output_bias, first_gain, first_shift, inner_weight, inner_bias, outer_weight, outer_bias, second_gain, second_shift)))
    inputs = tokens.astype(jnp.float32)
    slot_count = inputs.shape[0] // SEQ_LEN
    input_nudge = jnp.zeros_like(inputs)

    def forward(inputs_all, nudge_all, weights_all):

        def slot_step(running, pieces):
            slot_inputs, slot_nudge, lengths_row = pieces
            first_layer = layer_forward(slot_inputs, tuple((member[0] for member in weights_all)), lengths_row)
            passed = low_back(low(first_layer)) + slot_nudge
            second_layer = layer_forward(passed, tuple((member[1] for member in weights_all)), lengths_row)
            return (running, (first_layer, second_layer))
        shaped = (inputs_all.reshape(slot_count, SEQ_LEN, D), nudge_all.reshape(slot_count, SEQ_LEN, D), seq_lengths)
        running, outputs = lax.scan(jax.checkpoint(slot_step), jnp.zeros((), jnp.float32), shaped)
        return (outputs[0].reshape(-1, D), outputs[1].reshape(-1, D))
    primal, pullback = jax.vjp(forward, inputs, input_nudge, params)
    grad_inputs, grad_nudge, grads = pullback((jnp.zeros_like(primal[0]), cotangent.astype(jnp.float32)))
    layer_outputs = jnp.stack([primal[0], primal[1]]).astype(jnp.bfloat16)
    input_grads = jnp.stack([grad_inputs, grad_nudge])
    return (layer_outputs, input_grads, grads[0], grads[1], grads[2], grads[3], grads[4], grads[5], grads[6], grads[7], grads[8], grads[9], grads[10], grads[11], grads[12], grads[13], grads[14], grads[15])
```

```python
import functools
import math

import jax
import jax.numpy as jnp
import numpy as np
from jax import lax
from jax.experimental import pallas as pl
from jax.experimental.pallas import tpu as pltpu
from jax.sharding import PartitionSpec as P

D = 384
HEADS = 6
HEAD_DIM = 64
FF = 1536
SEQ_LEN = 512
MICRO = 2
COLS = FF // D

norm_eps = 1e-12
rope_base = 10000.0
far = -1e9

bf16 = jnp.bfloat16
f32 = jnp.float32

NT = (((1,), (1,)), ((), ()))
TN = (((0,), (0,)), ((), ()))

QB, KB, VB, OB, G1, S1, C1, C2, G2, S2 = 0, 1, 2, 3, 4, 5, 6, 10, 11, 12
SMALL = 16
AQ, ASMALL, AK, AV, AO = 0, 384, 448, 832, 1280
AROWS = 1664
FROWS = 2 * FF


def rotary_constants():
    places = np.arange(SEQ_LEN, dtype=np.float64)[:, None]
    pairs = (np.arange(128) // 2) % (HEAD_DIM // 2)
    angles = places * np.exp(pairs * (-2.0 * math.log(rope_base) / HEAD_DIM))[None, :]
    sign = np.where(np.arange(128) % 2 == 0, -1.0, 1.0)[None, :]
    return np.cos(angles).astype(np.float32), (np.sin(angles) * sign).astype(np.float32)


def dot(a, b):
    return jnp.dot(a, b, preferred_element_type=f32)


def dot_nt(a, b):
    return lax.dot_general(a, b, NT, preferred_element_type=f32)


def dot_tn(a, b):
    return lax.dot_general(a, b, TN, preferred_element_type=f32)


def segments(ends, places):
    return sum((places >= e).astype(jnp.int32) for e in ends)


def lane_iota(width=128):
    return lax.broadcasted_iota(jnp.int32, (SEQ_LEN, width), 1)


def turn(values, cos, sin):
    lane = lane_iota()
    parts = []
    for j in range(D // 128):
        u = values[:, j * 128 : (j + 1) * 128]
        partner = jnp.where(lane % 2 == 0, pltpu.roll(u, 127, 1), pltpu.roll(u, 1, 1))
        parts.append(u * cos + partner * sin)
    return jnp.concatenate(parts, axis=1)


def normalize(summed):
    centered = summed - jnp.mean(summed, axis=-1, keepdims=True)
    scale = lax.rsqrt(jnp.mean(centered * centered, axis=-1, keepdims=True) + norm_eps)
    return centered * scale, scale


def normalize_back(grad, normed, scale):
    return scale * (
        grad
        - jnp.mean(grad, axis=-1, keepdims=True)
        - normed * jnp.mean(grad * normed, axis=-1, keepdims=True)
    )


def marks(ends):
    lane = lane_iota() % HEAD_DIM
    rows = lax.broadcasted_iota(jnp.int32, (SEQ_LEN, 1), 0)
    own = lane == segments(ends, rows)
    query_marks = own.astype(f32).astype(bf16)
    key_marks = jnp.where(own | (lane > 4), 0.0, far).astype(bf16)
    return query_marks, key_marks


class Refs(dict):
    __getattr__ = dict.__getitem__


def read_ends(len_ref, block):
    ends, total = [], 0
    for j in range(4):
        total = total + len_ref[block, j]
        ends.append(total)
    return ends


def live_rows(ends):
    rows = lax.broadcasted_iota(jnp.int32, (SEQ_LEN, 1), 0)
    return (rows < ends[3]).astype(f32)


def forward(x, w, s, ends, h_ref):
    cos, sin = w.cos[...], w.sin[...]
    s.qb[...] = turn(dot(x, w.wq[...]) + w.bq[...].astype(f32), cos, sin).astype(bf16)
    s.kb[...] = turn(dot(x, w.wk[...]) + w.bk[...].astype(f32), cos, sin).astype(bf16)
    s.vb[...] = (dot(x, w.wv[...]) + w.bv[...].astype(f32)).astype(bf16)
    query_marks, key_marks = marks(ends)
    lane = lane_iota()
    zero = jnp.zeros((SEQ_LEN, 128), bf16)
    one = jnp.ones((SEQ_LEN, 128), bf16)
    scale = jnp.asarray(HEAD_DIM**-0.5, bf16)
    for pair in range(HEADS // 2):
        cols = slice(pair * 128, pair * 128 + 128)
        q2, k2, v2 = s.qb[:, cols] * scale, s.kb[:, cols], s.vb[:, cols]
        raised, tops, weighted = [], [], []
        for side in range(2):
            mine = (lane >= HEAD_DIM) == (side == 1)
            scores = dot_nt(jnp.where(mine, q2, query_marks), jnp.where(mine, k2, key_marks))
            top = jnp.max(scores, axis=-1, keepdims=True)
            raised.append(jnp.exp(scores - top).astype(bf16))
            tops.append(top)
            weighted.append(jnp.concatenate([jnp.where(mine, v2, zero), jnp.where(mine, one, zero)], axis=1))
        both = dot(jnp.concatenate(raised, axis=1), jnp.concatenate(weighted, axis=0))
        total = both[:, 128:]
        s.cb[:, cols] = (both[:, :128] / total).astype(bf16)
        log_total = jnp.log(total)
        s.st[:, 2 * pair : 2 * pair + 1] = tops[0] + log_total[:, 0:1]
        s.st[:, 2 * pair + 1 : 2 * pair + 2] = tops[1] + log_total[:, HEAD_DIM : HEAD_DIM + 1]
    attended = dot(s.cb[...], w.wo[...]) + w.bo[...].astype(f32)
    n1, r1 = normalize(x.astype(f32) + attended)
    s.n1[...] = n1
    s.st[:, 8:9] = r1
    u1 = n1 * w.g1[...].astype(f32) + w.s1[...].astype(f32)
    ub = u1.astype(bf16)
    s.ub[...] = ub
    total = u1 + w.c2[...].astype(f32)
    for j in range(COLS):
        cols = slice(j * D, (j + 1) * D)
        z = dot(ub, w.w1[:, cols]) + w.c1[:, cols].astype(f32)
        below = 0.5 + 0.5 * lax.erf(z * 0.7071067811865476)
        gb = (z * below).astype(bf16)
        s.gb[:, cols] = gb
        s.gp[:, cols] = (below + z * (jnp.exp(-0.5 * z * z) * 0.3989422804014327)).astype(bf16)
        total = total + dot(gb, w.w2[cols, :])
    n2, r2 = normalize(total)
    s.n2[...] = n2
    s.st[:, 9:10] = r2
    result = (n2 * w.g2[...].astype(f32) + w.s2[...].astype(f32)) * live_rows(ends)
    h_ref[...] = result.astype(bf16)


def column_sum(values):
    return jnp.sum(values, axis=0, keepdims=True)


def ffn_back(grad, w, s, t, ends):
    grad = grad * live_rows(ends)
    n2 = s.n2[...]
    t.sm[G2 : G2 + 1, :] = column_sum(grad * n2)
    t.sm[S2 : S2 + 1, :] = column_sum(grad)
    ds2 = normalize_back(grad * w.g2[...].astype(f32), n2, s.st[:, 9:10])
    df = ds2.astype(bf16)
    t.df[...] = df
    t.sm[C2 : C2 + 1, :] = column_sum(df.astype(f32))
    du1 = ds2
    for j in range(COLS):
        cols = slice(j * D, (j + 1) * D)
        dz = (dot_nt(df, w.w2[cols, :]) * s.gp[:, cols].astype(f32)).astype(bf16)
        t.dz[:, cols] = dz
        t.sm[C1 + j : C1 + j + 1, :] = column_sum(dz.astype(f32))
        du1 = du1 + dot_nt(dz, w.w1[:, cols])
    n1 = s.n1[...]
    t.sm[G1 : G1 + 1, :] = column_sum(du1 * n1)
    t.sm[S1 : S1 + 1, :] = column_sum(du1)
    ds1 = normalize_back(du1 * w.g1[...].astype(f32), n1, s.st[:, 8:9])
    t.ds1[...] = ds1
    da = ds1.astype(bf16)
    t.da[...] = da
    t.sm[OB : OB + 1, :] = column_sum(da.astype(f32))


def attention_back(w, s, t, ends, dh_ref, dhb_ref):
    t.dc[...] = dot_nt(t.da[...], w.wo[...]).astype(bf16)
    query_marks, key_marks = marks(ends)
    lane = lane_iota()
    zero = jnp.zeros((SEQ_LEN, 128), bf16)
    scale = jnp.asarray(HEAD_DIM**-0.5, bf16)
    cos, sin = w.cos[...], w.sin[...]
    first = lane < HEAD_DIM
    for pair in range(HEADS // 2):
        cols = slice(pair * 128, pair * 128 + 128)
        q2, k2, v2, dc2 = s.qb[:, cols] * scale, s.kb[:, cols], s.vb[:, cols], t.dc[:, cols]
        grads, dks, dvs = [], [], []
        for side in range(2):
            head = 2 * pair + side
            mine = (lane >= HEAD_DIM) == (side == 1)
            scores = dot_nt(jnp.where(mine, q2, query_marks), jnp.where(mine, k2, key_marks))
            shares = jnp.exp(scores - s.st[:, head : head + 1])
            grad_shares = dot_nt(jnp.where(mine, dc2, zero), v2)
            row = jnp.sum(shares * grad_shares, axis=-1, keepdims=True)
            grad_scores = (shares * (grad_shares - row)).astype(bf16)
            grads.append(grad_scores)
            dvs.append(dot_tn(shares.astype(bf16), dc2))
            dks.append(dot_tn(grad_scores, q2))
        k2s = k2 * scale
        keys = jnp.concatenate([jnp.where(first, k2s, zero), jnp.where(first, zero, k2s)], axis=0)
        dq = dot(jnp.concatenate(grads, axis=1), keys)
        dk = jnp.where(first, dks[0], dks[1])
        dv = jnp.where(first, dvs[0], dvs[1])

        def back(u):
            partner = jnp.where(lane % 2 == 0, pltpu.roll(u, 127, 1), pltpu.roll(u, 1, 1))
            return (u * cos - partner * sin).astype(bf16)

        t.dq[:, cols] = back(dq)
        t.dk[:, cols] = back(dk)
        t.dv[:, cols] = dv.astype(bf16)
    dq, dk, dv = t.dq[...], t.dk[...], t.dv[...]
    t.sm[QB : QB + 1, :] = column_sum(dq.astype(f32))
    t.sm[KB : KB + 1, :] = column_sum(dk.astype(f32))
    t.sm[VB : VB + 1, :] = column_sum(dv.astype(f32))
    dh = t.ds1[...] + dot_nt(dq, w.wq[...]) + dot_nt(dk, w.wk[...]) + dot_nt(dv, w.wv[...])
    dh_ref[...] = dh
    if dhb_ref is not None:
        dhb_ref[...] = dh.astype(bf16)


def ffn_terms(sets, start, out_ref):
    for j in range(COLS):
        cols = slice(j * D, (j + 1) * D)
        rows = slice(j * D, (j + 1) * D)
        total = sum(dot_tn(t.ub[...], t.dz[:, cols]) for t in sets)
        if start is not None:
            total = total + start[rows, :]
        out_ref[rows, :] = total.astype(out_ref.dtype)
        rows = slice(FF + j * D, FF + (j + 1) * D)
        total = sum(dot_tn(t.gb[:, cols], t.df[...]) for t in sets)
        if start is not None:
            total = total + start[rows, :]
        out_ref[rows, :] = total.astype(out_ref.dtype)


def attention_terms(sets, start, out_ref):
    for row, left, right in ((AQ, "x", "dq"), (AK, "x", "dk"), (AV, "x", "dv"), (AO, "cb", "da")):
        rows = slice(row, row + D)
        total = sum(dot_tn(t[left][...], t[right][...]) for t in sets)
        if start is not None:
            total = total + start[rows, :]
        out_ref[rows, :] = total.astype(out_ref.dtype)


def small_terms(smalls, out_ref):
    out_ref[ASMALL : ASMALL + SMALL, :] = sum(m[...] for m in smalls).astype(out_ref.dtype)
    out_ref[ASMALL + SMALL : AK, :] = jnp.zeros((AK - ASMALL - SMALL, D), out_ref.dtype)
    out_ref[AV + D : AO, :] = jnp.zeros((AO - AV - D, D), out_ref.dtype)


WNAMES = ("wq", "bq", "wk", "bk", "wv", "bv", "wo", "bo", "g1", "s1", "w1", "c1", "w2", "c2", "g2", "s2")
ROW = jax.ShapeDtypeStruct((SEQ_LEN, D), bf16)
ROWF = jax.ShapeDtypeStruct((SEQ_LEN, D), f32)
WIDE = jax.ShapeDtypeStruct((SEQ_LEN, FF), bf16)
STAT = jax.ShapeDtypeStruct((SEQ_LEN, 128), f32)
STATE = dict(qb=ROW, kb=ROW, vb=ROW, cb=ROW, ub=ROW, gb=WIDE, gp=WIDE, n1=ROWF, n2=ROWF, st=STAT)
STEP = dict(df=ROW, dz=WIDE, ds1=ROWF, da=ROW, dc=ROW, dq=ROW, dk=ROW, dv=ROW)
SMALLS = jax.ShapeDtypeStruct((SMALL, D), f32)


def kernel_call(body, role, name, section, lengths, ins, outs, scratch=None, aliases=None, vmem_mib=40):
    scratch = scratch or {}
    in_names, out_names, scratch_names = list(ins), list(outs), list(scratch)

    def kernel(sec_ref, len_ref, *refs):
        named = Refs(zip(in_names, refs))
        rest = refs[len(in_names) :]
        named.update(zip(out_names, rest))
        named.update(zip(scratch_names, rest[len(out_names) :]))

        def run():
            body(len_ref, named)

        if role is None:
            run()
        else:
            pl.when(sec_ref[0] == role)(run)

    smem = pl.BlockSpec(memory_space=pltpu.SMEM)
    vmem = pl.BlockSpec(memory_space=pltpu.VMEM)
    results = pl.pallas_call(
        kernel,
        out_shape=[outs[n] for n in out_names],
        in_specs=[smem, smem] + [vmem] * len(in_names),
        out_specs=[vmem] * len(out_names),
        scratch_shapes=[pltpu.VMEM(scratch[n].shape, scratch[n].dtype) for n in scratch_names],
        input_output_aliases={
            2 + in_names.index(i): out_names.index(o) for i, o in (aliases or {}).items()
        },
        compiler_params=pltpu.CompilerParams(vmem_limit_bytes=vmem_mib * 1024 * 1024),
        name=name,
    )(section, lengths, *[ins[n] for n in in_names])
    return Refs(zip(out_names, results))


def pick(refs, names):
    return Refs((n, refs[n]) for n in names)


def rows_of(ref, block):
    return ref[block * SEQ_LEN : (block + 1) * SEQ_LEN, :]


def exchange(block, axis, bit):
    n = lax.axis_size(axis)
    return lax.ppermute(block, axis, [(i, i ^ (1 << bit)) for i in range(n)])


def shifted(block, axis, distance):
    devices = range(lax.axis_size(axis))
    route = [(i - distance, i) for i in devices if i - distance in devices]
    return lax.ppermute(block, axis, route)


def reduce_step(block, bit, index):
    half = block.shape[0] // 2
    side = (index >> bit) & 1
    away = lax.dynamic_slice_in_dim(block, (1 - side) * half, half, 0)
    kept = lax.dynamic_slice_in_dim(block, side * half, half, 0)
    return (kept.astype(f32) + exchange(away, "dp", bit).astype(f32)).astype(bf16)


def gather_step(block, bit, index):
    side = (index >> bit) & 1
    other = exchange(block, "dp", bit)
    return jnp.where(side == 0, jnp.concatenate([block, other]), jnp.concatenate([other, block]))


def summed_halves(buffer, cut):
    n = lax.axis_size("dp")
    bits = n.bit_length() - 1
    index = lax.axis_index("dp")
    mine = reduce_step(buffer, 0, index)
    orders = [list(range(1, bits)), list(range(1, bits))]
    if bits > 2:
        orders[1][0], orders[1][1] = orders[1][1], orders[1][0]
    parts = [mine[:cut], mine[cut:]]
    for step in range(bits - 1):
        for k in range(2):
            parts[k] = reduce_step(parts[k], orders[k][step], index)
    for step in reversed(range(bits - 1)):
        for k in range(2):
            parts[k] = gather_step(parts[k], orders[k][step], index)
    mine = jnp.concatenate(parts)
    return mine, exchange(mine, "dp", 0)


def assemble_ffn(core, mine, other):
    def kernel(core_ref, mine_ref, other_ref, inner_ref, outer_ref):
        def write(low, high):
            for j in range(COLS):
                inner_ref[0, :, j * D : (j + 1) * D] = low[j * D : (j + 1) * D, :].astype(f32)
            outer_ref[0] = high[...].astype(f32)

        pl.when(core_ref[0] == 0)(lambda: write(mine_ref, other_ref))
        pl.when(core_ref[0] == 1)(lambda: write(other_ref, mine_ref))

    vmem = pl.BlockSpec(memory_space=pltpu.VMEM)
    return pl.pallas_call(
        kernel,
        out_shape=[jax.ShapeDtypeStruct((1, D, FF), f32), jax.ShapeDtypeStruct((1, FF, D), f32)],
        in_specs=[pl.BlockSpec(memory_space=pltpu.SMEM), vmem, vmem],
        out_specs=[vmem] * 2,
        name="assemble_ffn",
    )(core, mine, other)


def assemble_attention(core, mine, other):
    def kernel(core_ref, mine_ref, other_ref, wq, wk, wv, wo, bq, bk, bv, bo, g1, s1, c1, c2, g2, s2):
        def write(low, high):
            wq[0] = low[AQ : AQ + D, :].astype(f32)
            wk[0] = low[AK : AK + D, :].astype(f32)
            wv[0] = high[AV - AV : AV - AV + D, :].astype(f32)
            wo[0] = high[AO - AV : AO - AV + D, :].astype(f32)
            small = low[ASMALL : ASMALL + SMALL, :].astype(f32)
            for ref, row in ((bq, QB), (bk, KB), (bv, VB), (bo, OB), (g1, G1), (s1, S1), (c2, C2), (g2, G2), (s2, S2)):
                ref[...] = small[row : row + 1, :]
            for j in range(COLS):
                c1[:, j * D : (j + 1) * D] = small[C1 + j : C1 + j + 1, :]

        pl.when(core_ref[0] == 0)(lambda: write(mine_ref, other_ref))
        pl.when(core_ref[0] == 1)(lambda: write(other_ref, mine_ref))

    vmem = pl.BlockSpec(memory_space=pltpu.VMEM)
    square = jax.ShapeDtypeStruct((1, D, D), f32)
    line = jax.ShapeDtypeStruct((1, D), f32)
    shapes = [square] * 4 + [line] * 6 + [jax.ShapeDtypeStruct((1, FF), f32)] + [line] * 3
    return pl.pallas_call(
        kernel,
        out_shape=shapes,
        in_specs=[pl.BlockSpec(memory_space=pltpu.SMEM), vmem, vmem],
        out_specs=[vmem] * len(shapes),
        name="assemble_attention",
    )(core, mine, other)


def local(tokens, cotangent, lengths, *weights):
    section = lax.axis_index("section").astype(jnp.int32).reshape(1)
    core = (lax.axis_index("dp") & 1).astype(jnp.int32).reshape(1)
    cos, sin = rotary_constants()
    w = dict(zip(WNAMES, (m[0] if m.ndim == 3 else m for m in weights)))
    tables = dict(cos=jnp.asarray(cos), sin=jnp.asarray(sin))
    call = functools.partial(kernel_call, section=section, lengths=lengths)

    def first_forward(block):
        def body(len_ref, r):
            forward(rows_of(r.tokens, block), r, r, read_ends(len_ref, block), r.h)

        return call(
            body, 0, f"first_forward_{block}", ins=dict(tokens=tokens, **w, **tables), outs=dict(h=ROW, **STATE)
        )

    def second_layer(block, x):
        def body(len_ref, r):
            ends = read_ends(len_ref, block)
            forward(r.x[...], r, r, ends, r.h)
            ffn_back(rows_of(r.cotangent, block), r, r, r, ends)
            attention_back(r, r, r, ends, r.dh, r.dhb)

        kept = ("cb", "ub", "gb", "df", "dz", "da", "dq", "dk", "dv")
        every = dict(**STATE, **STEP)
        return call(
            body,
            1,
            f"second_layer_{block}",
            ins=dict(x=x, cotangent=cotangent, **w, **tables),
            outs=dict(h=ROW, dh=ROWF, dhb=ROW, sm=SMALLS, **{n: every[n] for n in kept}),
            scratch={n: every[n] for n in every if n not in kept},
        )

    f0 = first_forward(0)
    x0 = shifted(f0.h, "section", 1)
    f1 = first_forward(1)
    x1 = shifted(f1.h, "section", 1)
    s0 = second_layer(0, x0)
    g0 = shifted(s0.dhb, "section", -1)
    s1 = second_layer(1, x1)
    g1 = shifted(s1.dhb, "section", -1)

    def second_ffn(len_ref, r):
        sets = [Refs((n, r[n + str(b)]) for n in ("ub", "dz", "gb", "df")) for b in range(MICRO)]
        ffn_terms(sets, None, r.ffn)

    ffn = call(
        second_ffn,
        1,
        "second_ffn",
        ins={n + str(b): s[n] for b, s in enumerate((s0, s1)) for n in ("ub", "dz", "gb", "df")},
        outs=dict(ffn=jax.ShapeDtypeStruct((FROWS, D), bf16)),
    ).ffn

    def second_attention(len_ref, r):
        sets = [Refs((n, r[n + str(b)]) for n in ("x", "dq", "dk", "dv", "cb", "da")) for b in range(MICRO)]
        attention_terms(sets, None, r.att)
        small_terms([r.sm0, r.sm1], r.att)

    att = call(
        second_attention,
        1,
        "second_attention",
        ins=dict(
            x0=x0,
            x1=x1,
            **{
                n + str(b): s[n]
                for b, s in enumerate((s0, s1))
                for n in ("dq", "dk", "dv", "cb", "da", "sm")
            },
        ),
        outs=dict(att=jax.ShapeDtypeStruct((AROWS, D), bf16)),
    ).att

    def first_backward_0(len_ref, r):
        ends = read_ends(len_ref, 0)
        ffn_back(r.grad[...].astype(f32), r, r, r, ends)
        ffn_terms([r], None, r.ffn)
        attention_back(r, r, r, ends, r.dh, None)
        r["x"] = r.tokens.at[pl.ds(0, SEQ_LEN)]
        attention_terms([r], None, r.att)

    b0 = call(
        first_backward_0,
        0,
        "first_backward_0",
        ins=dict(grad=g0, tokens=tokens, **pick(f0, STATE), **w, **tables),
        outs=dict(
            dh=ROWF,
            sm=SMALLS,
            ffn=jax.ShapeDtypeStruct((FROWS, D), f32),
            att=jax.ShapeDtypeStruct((AROWS, D), f32),
        ),
        scratch=STEP,
    )

    def first_ffn_1(len_ref, r):
        ffn_back(r.grad[...].astype(f32), r, r, r, read_ends(len_ref, 1))
        ffn_terms([r], r.start, r.ffn)

    names = ("ub", "gb", "gp", "n1", "n2", "st")
    b1 = call(
        first_ffn_1,
        0,
        "first_ffn_1",
        ins=dict(grad=g1, start=b0.ffn, before=ffn, **pick(f1, names), **w),
        outs=dict(ffn=jax.ShapeDtypeStruct((FROWS, D), bf16), ds1=ROWF, da=ROW, sm=SMALLS),
        scratch=dict(df=ROW, dz=WIDE),
        aliases=dict(before="ffn"),
    )
    inner_outer = summed_halves(b1.ffn, FF // 2)

    def first_attention_1(len_ref, r):
        r.sm[...] = r.sm_in[...]
        attention_back(r, r, r, read_ends(len_ref, 1), r.dh, None)
        r["x"] = r.tokens.at[pl.ds(SEQ_LEN, SEQ_LEN)]
        attention_terms([r], r.start, r.att)
        small_terms([r.sm, r.sm0], r.att)

    names = ("qb", "kb", "vb", "cb", "st")
    b2 = call(
        first_attention_1,
        0,
        "first_attention_1",
        ins=dict(
            tokens=tokens,
            ds1=b1.ds1,
            da=b1.da,
            sm_in=b1.sm,
            sm0=b0.sm,
            start=b0.att,
            before=att,
            **pick(f1, names),
            **w,
            **tables,
        ),
        outs=dict(att=jax.ShapeDtypeStruct((AROWS, D), bf16), dh=ROWF),
        scratch=dict(dc=ROW, dq=ROW, dk=ROW, dv=ROW, sm=SMALLS),
        aliases=dict(before="att"),
    )
    others = summed_halves(b2.att, ASMALL + 64)

    is_first = section[0] == 0
    layer_rows = jnp.concatenate([jnp.where(is_first, f0.h, s0.h), jnp.where(is_first, f1.h, s1.h)])
    grad_rows = jnp.concatenate([jnp.where(is_first, b0.dh, s0.dh), jnp.where(is_first, b2.dh, s1.dh)])
    inner, outer = assemble_ffn(core, *inner_outer)
    wq, wk, wv, wo, bq, bk, bv, bo, g1_, s1_, c1, c2, g2, s2 = assemble_attention(core, *others)
    return (
        layer_rows[None],
        grad_rows[None],
        wq,
        bq,
        wk,
        bk,
        wv,
        bv,
        wo,
        bo,
        g1_,
        s1_,
        inner,
        c1,
        outer,
        c2,
        g2,
        s2,
    )


def solution(mesh):
    square, line = P("section", None, None), P("section", None)
    weights = (square, line) * 4 + (line, line) + (square, line) * 2 + (line, line)
    rows = P("section", "dp", None)
    return jax.shard_map(
        local,
        mesh=mesh,
        in_specs=(P("dp", None),) * 3 + weights,
        out_specs=(rows, rows) + weights,
        check_vma=False,
    )
```

```python
import functools
import itertools
import math

import jax
import jax.numpy as jnp
import numpy as np
from jax import lax
from jax.experimental import pallas as pl
from jax.experimental.pallas import tpu as pltpu
from jax.sharding import PartitionSpec as P

D = 384
HEADS = 6
HEAD_DIM = 64
FF = 1536
SEQ_LEN = 512
MICRO = 2
COLS = FF // D

norm_eps = 1e-12
rope_base = 10000.0
far = -1e9

bf16 = jnp.bfloat16
f32 = jnp.float32

NT = (((1,), (1,)), ((), ()))
TN = (((0,), (0,)), ((), ()))

QB, KB, VB, OB, G1, S1, C1, C2, G2, S2 = 0, 1, 2, 3, 4, 5, 6, 10, 11, 12
SMALL = 16
W1, OA, W2, OB2 = 0, 1536, 1728, 3264
FROWS, FCUTS = 3456, (896, 1728)
AQ, VA, ASMALL, AK, VB2 = 0, 384, 576, 640, 1024
AROWS, ACUTS = 1280, (640,)


def rotary_constants():
    places = np.arange(SEQ_LEN, dtype=np.float64)[:, None]
    pairs = (np.arange(128) // 2) % (HEAD_DIM // 2)
    angles = places * np.exp(pairs * (-2.0 * math.log(rope_base) / HEAD_DIM))[None, :]
    sign = np.where(np.arange(128) % 2 == 0, -1.0, 1.0)[None, :]
    return np.cos(angles).astype(np.float32), (np.sin(angles) * sign).astype(np.float32)


def dot(a, b):
    return jnp.dot(a, b, preferred_element_type=f32)


def dot_nt(a, b):
    return lax.dot_general(a, b, NT, preferred_element_type=f32)


def dot_tn(a, b):
    return lax.dot_general(a, b, TN, preferred_element_type=f32)


def segments(ends, places):
    return sum((places >= e).astype(jnp.int32) for e in ends)


def lane_iota(width=128):
    return lax.broadcasted_iota(jnp.int32, (SEQ_LEN, width), 1)


def turn(values, cos, sin):
    lane = lane_iota()
    parts = []
    for j in range(D // 128):
        u = values[:, j * 128 : (j + 1) * 128]
        partner = jnp.where(lane % 2 == 0, pltpu.roll(u, 127, 1), pltpu.roll(u, 1, 1))
        parts.append(u * cos + partner * sin)
    return jnp.concatenate(parts, axis=1)


def normalize(summed):
    centered = summed - jnp.mean(summed, axis=-1, keepdims=True)
    scale = lax.rsqrt(jnp.mean(centered * centered, axis=-1, keepdims=True) + norm_eps)
    return centered * scale, scale


def normalize_back(grad, normed, scale):
    return scale * (
        grad
        - jnp.mean(grad, axis=-1, keepdims=True)
        - normed * jnp.mean(grad * normed, axis=-1, keepdims=True)
    )


def marks(ends):
    lane = lane_iota() % HEAD_DIM
    rows = lax.broadcasted_iota(jnp.int32, (SEQ_LEN, 1), 0)
    own = lane == segments(ends, rows)
    query_marks = own.astype(f32).astype(bf16)
    key_marks = jnp.where(own | (lane > 4), 0.0, far).astype(bf16)
    return query_marks, key_marks


class Refs(dict):
    __getattr__ = dict.__getitem__


def read_ends(len_ref, block):
    ends, total = [], 0
    for j in range(4):
        total = total + len_ref[block, j]
        ends.append(total)
    return ends


def live_rows(ends):
    rows = lax.broadcasted_iota(jnp.int32, (SEQ_LEN, 1), 0)
    return (rows < ends[3]).astype(f32)


def lanes(index, width):
    if isinstance(index, int):
        return slice(index * width, (index + 1) * width)
    return pl.ds(pl.multiple_of(index * width, width), width)


F_COMPACT = (False, True)
B_COMPACT = (True, True)


def repeat(steps, step, compact):
    if compact:

        def body(j, carry):
            step(j)
            return carry

        lax.fori_loop(steps[0], steps[-1] + 1, body, 0)
    else:
        for j in steps:
            step(j)


def line(r, name):
    row = LINES[name]
    return r.lines[row : row + 1, :]


def forward(r, ends, h_ref, compact=False):
    r.need("x", "lines", "wq", "cos", "sin")
    x, cos, sin = r.x[...], r.cos[...], r.sin[...]
    r.qb[...] = turn(dot(x, r.wq[...]) + line(r, "bq"), cos, sin).astype(bf16)
    r.need("wk")
    r.kb[...] = turn(dot(x, r.wk[...]) + line(r, "bk"), cos, sin).astype(bf16)
    r.need("wv")
    r.vb[...] = (dot(x, r.wv[...]) + line(r, "bv")).astype(bf16)
    r.keep("qb", "kb", "vb")
    query_marks, key_marks = marks(ends)

    def attend(pair):
        lane = lane_iota()
        zero = jnp.zeros((SEQ_LEN, 128), bf16)
        one = jnp.ones((SEQ_LEN, 128), bf16)
        cols = lanes(pair, 128)
        q2, k2, v2 = r.qb[:, cols] * jnp.asarray(HEAD_DIM**-0.5, bf16), r.kb[:, cols], r.vb[:, cols]
        raised, tops, weighted = [], [], []
        for side in range(2):
            mine = (lane >= HEAD_DIM) == (side == 1)
            scores = dot_nt(jnp.where(mine, q2, query_marks), jnp.where(mine, k2, key_marks))
            top = jnp.max(scores, axis=-1, keepdims=True)
            raised.append(jnp.exp(scores - top).astype(bf16))
            tops.append(top)
            weighted.append(jnp.concatenate([jnp.where(mine, v2, zero), jnp.where(mine, one, zero)], axis=1))
        both = dot(jnp.concatenate(raised, axis=1), jnp.concatenate(weighted, axis=0))
        total = both[:, 128:]
        r.cb[:, cols] = (both[:, :128] / total).astype(bf16)
        log_total = jnp.log(total)
        for side in range(2):
            value = tops[side] + log_total[:, side * HEAD_DIM : side * HEAD_DIM + 1]
            r.stats[...] = jnp.where(lane == 2 * pair + side, value, r.stats[...])

    repeat(range(HEADS // 2), attend, compact)
    r.lse[...] = r.stats[...].T[:8]
    r.keep("cb", "lse")
    r.need("wo")
    attended = dot(r.cb[...], r.wo[...]) + line(r, "bo")
    n1, r1 = normalize(x.astype(f32) + attended)
    r.n1[...] = n1
    u1 = n1 * line(r, "g1") + line(r, "s1")
    r.ub[...] = u1.astype(bf16)
    r.keep("n1", "ub")
    r.total[...] = u1 + line(r, "c2")
    r.need("w1", "w2")

    def widen(j):
        cols = lanes(j, D)
        z = dot(r.ub[...], r.w1[:, cols]) + r.lines[pl.ds(LINES["c1"] + j, 1), :]
        below = 0.5 + 0.5 * lax.erf(z * 0.7071067811865476)
        gb = (z * below).astype(bf16)
        r.gb[:, cols] = gb
        r.gp[:, cols] = (below + z * (jnp.exp(-0.5 * z * z) * 0.3989422804014327)).astype(bf16)
        if not compact:
            r.keep("gb", "gp", cols=cols)
        r.total[...] += dot(gb, r.w2[lanes(j, D), :])

    repeat(range(COLS), widen, compact)
    if compact:
        r.keep("gb", "gp")
    n2, r2 = normalize(r.total[...])
    r.n2[...] = n2
    lane = lane_iota()
    r.scales[...] = jnp.where(lane == 0, r1, r2)
    h_ref[...] = ((n2 * line(r, "g2") + line(r, "s2")) * live_rows(ends)).astype(bf16)
    r.keep("n2", "scales")


def column_sum(values):
    return jnp.sum(values, axis=0, keepdims=True)


def ffn_back(grad, r, ends):
    grad = grad * live_rows(ends)
    r.need("n2", "scales", "lines")
    n2 = r.n2[...]
    r.sm[G2 : G2 + 1, :] = column_sum(grad * n2)
    r.sm[S2 : S2 + 1, :] = column_sum(grad)
    ds2 = normalize_back(grad * line(r, "g2"), n2, r.scales[:, 1:2])
    df = ds2.astype(bf16)
    r.df[...] = df
    r.sm[C2 : C2 + 1, :] = column_sum(df.astype(f32))
    r.total[...] = ds2
    r.keep("df")
    r.need("w1", "w2", "gp")

    def narrow(j):
        cols = lanes(j, D)
        dz = (dot_nt(r.df[...], r.w2[lanes(j, D), :]) * r.gp[:, cols].astype(f32)).astype(bf16)
        r.dz[:, cols] = dz
        r.keep("dz", cols=cols)
        r.sm[C1 + j : C1 + j + 1, :] = column_sum(dz.astype(f32))
        r.total[...] += dot_nt(dz, r.w1[:, cols])

    for j in range(COLS):
        narrow(j)
    r.need("n1")
    du1, n1 = r.total[...], r.n1[...]
    r.sm[G1 : G1 + 1, :] = column_sum(du1 * n1)
    r.sm[S1 : S1 + 1, :] = column_sum(du1)
    ds1 = normalize_back(du1 * line(r, "g1"), n1, r.scales[:, 0:1])
    r.ds1[...] = ds1
    da = ds1.astype(bf16)
    r.da[...] = da
    r.sm[OB : OB + 1, :] = column_sum(da.astype(f32))
    r.keep("da", "ds1")


def attention_back(r, ends, pairs=(0, 1, 2), compact=False):
    if 0 in pairs:
        r.need("da", "wo")
        r.dc[...] = dot_nt(r.da[...], r.wo[...]).astype(bf16)
    query_marks, key_marks = marks(ends)
    r.need("qb", "kb", "vb", "lse", "cos", "sin")

    def attend(pair):
        lane = lane_iota()
        first = lane < HEAD_DIM
        zero = jnp.zeros((SEQ_LEN, 128), bf16)
        scale = jnp.asarray(HEAD_DIM**-0.5, bf16)
        cos, sin = r.cos[...], r.sin[...]
        cols = lanes(pair, 128)
        q2, k2, v2, dc2 = r.qb[:, cols] * scale, r.kb[:, cols], r.vb[:, cols], r.dc[:, cols]
        grads, dks, dvs = [], [], []
        for side in range(2):
            head = 2 * pair + side
            mine = (lane >= HEAD_DIM) == (side == 1)
            scores = dot_nt(jnp.where(mine, k2, key_marks), jnp.where(mine, q2, query_marks))
            shares = jnp.exp(scores - r.lse[pl.ds(head, 1), :])
            grad_shares = dot_nt(jnp.where(mine, v2, zero), dc2)
            row = jnp.sum(shares * grad_shares, axis=0, keepdims=True)
            grad_scores = (shares * (grad_shares - row)).astype(bf16)
            grads.append(grad_scores)
            dvs.append(dot(shares.astype(bf16), dc2))
            dks.append(dot(grad_scores, q2))
        k2s = k2 * scale
        keys = jnp.concatenate([jnp.where(first, k2s, zero), jnp.where(first, zero, k2s)], axis=0)
        dq = dot(keys.T, jnp.concatenate(grads, axis=0)).T
        dk = jnp.where(first, dks[0], dks[1])

        def back(u):
            partner = jnp.where(lane % 2 == 0, pltpu.roll(u, 127, 1), pltpu.roll(u, 1, 1))
            return (u * cos - partner * sin).astype(bf16)

        r.dq[:, cols] = back(dq)
        r.dk[:, cols] = back(dk)
        r.dv[:, cols] = jnp.where(first, dvs[0], dvs[1]).astype(bf16)
        if not compact:
            r.keep("dq", "dk", "dv", cols=cols)

    repeat(pairs, attend, compact)
    if HEADS // 2 - 1 not in pairs:
        return
    if compact:
        r.keep("dq", "dk", "dv")
    dq, dk, dv = r.dq[...], r.dk[...], r.dv[...]
    r.need("ds1", "wq", "wk", "wv")
    dh = r.ds1[...] + dot_nt(dq, r.wq[...]) + dot_nt(dk, r.wk[...]) + dot_nt(dv, r.wv[...])
    r.dh[...] = dh
    r.keep("dh")
    if "dhb" in r:
        r.dhb[...] = dh.astype(bf16)
    r.sm[QB : QB + 1, :] = column_sum(dq.astype(f32))
    r.sm[KB : KB + 1, :] = column_sum(dk.astype(f32))
    r.sm[VB : VB + 1, :] = column_sum(dv.astype(f32))


def add_up(total, start, out_ref, *places):
    for row, first, last in places:
        rows = slice(row, row + last - first)
        value = total[first:last]
        if start is not None:
            value = value + start[rows, :]
        out_ref[rows, :] = value.astype(out_ref.dtype)


def ffn_terms(r, sets, start, out_ref, sent=False):
    for k, (ub, dz, gb, df, cb, da) in enumerate(sets):
        r.need(ub, dz, cb, da)
        r.turned[k] = r[ub][...].T

    def half(k):
        if sent:
            r.keep_either(r.core == 1 - k, "kept", "away", out_ref.at[pl.ds(k * W2, W2)])

    total = sum(dot_tn(r[s[4]][...], r[s[5]][...]) for s in sets)
    add_up(total, start, out_ref, (OA, 0, D // 2), (OB2, D // 2, D))
    for j in range(COLS):
        cols = lanes(j, D)
        total = sum(dot(r.turned[k], r[s[1]][:, cols]) for k, s in enumerate(sets))
        add_up(total, start, out_ref, (W1 + j * D, 0, D))
    half(0)
    for s in sets:
        r.need(s[2], s[3])
    for j in range(COLS):
        cols = lanes(j, D)
        total = sum(dot_tn(r[s[2]][:, cols], r[s[3]][...]) for s in sets)
        add_up(total, start, out_ref, (W2 + j * D, 0, D))
    half(1)


def attention_terms(r, sets, smalls, start, out_ref, sent=False):
    for names in sets:
        r.need(*names)

    def half(k):
        if sent:
            r.keep_either(r.core == 1 - k, "kept", "away", out_ref.at[pl.ds(k * AK, AK)])

    def total(right):
        return sum(dot_tn(r[s[0]][...], r[s[right]][...]) for s in sets)

    add_up(total(3), start, out_ref, (VA, 0, D // 2), (VB2, D // 2, D))
    add_up(total(1), start, out_ref, (AQ, 0, D))
    if smalls:
        r.need(*smalls)
        values = sum(r[n][...] for n in smalls).astype(out_ref.dtype)
        rest = jnp.zeros((AK - ASMALL - SMALL, D), out_ref.dtype)
        out_ref[ASMALL:AK, :] = jnp.concatenate([values, rest])
        out_ref[VB2 + D // 2 : AROWS, :] = jnp.zeros((AROWS - VB2 - D // 2, D), out_ref.dtype)
    half(0)
    add_up(total(2), start, out_ref, (AK, 0, D))
    half(1)


WNAMES = ("wq", "bq", "wk", "bk", "wv", "bv", "wo", "bo", "g1", "s1", "w1", "c1", "w2", "c2", "g2", "s2")
LINES = dict(bq=0, bk=1, bv=2, bo=3, g1=4, s1=5, c1=6, c2=10, g2=11, s2=12)
ROW = jax.ShapeDtypeStruct((SEQ_LEN, D), bf16)
ROWF = jax.ShapeDtypeStruct((SEQ_LEN, D), f32)
WIDE = jax.ShapeDtypeStruct((SEQ_LEN, FF), bf16)
LSE = jax.ShapeDtypeStruct((8, SEQ_LEN), f32)
SCALES = jax.ShapeDtypeStruct((SEQ_LEN, 128), f32)
STATE = dict(qb=ROW, kb=ROW, vb=ROW, cb=ROW, lse=LSE, n1=ROWF, ub=ROW, gb=WIDE, gp=WIDE, n2=ROWF, scales=SCALES)
STEP = dict(df=ROW, dz=WIDE, ds1=ROWF, da=ROW, dc=ROW, dq=ROW, dk=ROW, dv=ROW)
SMALLS = jax.ShapeDtypeStruct((SMALL, D), f32)
TURNED = {n: jax.ShapeDtypeStruct((n, D, SEQ_LEN), bf16) for n in (1, 2)}


def kernel_call(
    body, role, name, section, core, lengths, loads=None, ins=None, fetched=None, vectors=None, stores=None, outs=None, scratch=None,
    aliases=None, vmem_mib=44, us=5
):
    loads, ins, stores, outs, scratch = (dict(d or {}) for d in (loads, ins, stores, outs, scratch))
    fetched, vectors, aliases = fetched or {}, vectors or {}, aliases or {}
    loads = {n: a if isinstance(a, tuple) else (a, None) for n, a in loads.items()}
    stores = {n: a if isinstance(a, tuple) else (a, None) for n, a in stores.items()}
    outs.update({n: jax.ShapeDtypeStruct(a.shape, a.dtype) for n, a in fetched.items()})
    if vectors:
        outs["lines"] = SMALLS

    def place(shape, block):
        return pltpu.VMEM((SEQ_LEN,) + shape.shape[1:] if block is not None else shape.shape, shape.dtype)

    def part(ref, block):
        return ref if block is None else ref.at[pl.ds(block * SEQ_LEN, SEQ_LEN)]

    hbm = pl.BlockSpec(memory_space=pltpu.HBM)
    vmem = pl.BlockSpec(memory_space=pltpu.VMEM)
    smem = pl.BlockSpec(memory_space=pltpu.SMEM)
    in_names = list(ins) + list(loads) + list(vectors) + list(fetched)
    out_names = list(stores) + list(outs)
    places = {n: place(a, b) for n, (a, b) in loads.items()}
    places.update({n: place(a, b) for n, (a, b) in stores.items() if n not in places})
    places.update({n: pltpu.VMEM(a.shape, a.dtype) for n, a in scratch.items()})
    places.update({n: pltpu.VMEM(a.shape, a.dtype) for n, a in vectors.items()})

    def kernel(sec_ref, core_ref, len_ref, *refs):
        given = dict(zip(in_names, refs))
        rest = refs[len(in_names) + len(aliases) :]
        results = dict(zip(out_names, rest))
        own = dict(zip(places, rest[len(out_names) :]))
        sems = refs[-1]
        r = Refs(own)
        for n in ins:
            r[n] = given[n]
        for n in outs:
            r[n] = results[n]
        used = itertools.count()
        waiting = {}

        def begin(source, target):
            copy = pltpu.make_async_copy(source, target, sems.at[next(used)])
            copy.start()
            return copy

        active = sec_ref[0] == role
        short = [begin(given[n], own[n]) for n in vectors]
        for n in fetched:
            waiting[n] = begin(given[n], results[n])
        everywhere = list(waiting.values())
        for n, copy in zip(vectors, short):
            copy.wait()
            for j in range(vectors[n].shape[1] // D):
                r.lines[LINES[n] + j : LINES[n] + j + 1, :] = own[n][:, j * D : (j + 1) * D].astype(f32)

        def run():
            for n, (_, block) in loads.items():
                waiting[n] = begin(part(given[n], block), own[n])
            sent = []

            def need(*names):
                for n in names:
                    if n in waiting:
                        waiting.pop(n).wait()

            def keep(*names, cols=None, source=None):
                for n in names:
                    if n in stores:
                        target, local = part(results[n], stores[n][1]), own[n] if source is None else source
                        if cols is not None:
                            target, local = target.at[:, cols], local.at[:, cols]
                        sent.append(begin(local, target))

            def keep_either(swap, first, second, source):
                k = next(used)
                copies = [pltpu.make_async_copy(source, results[n], sems.at[k]) for n in (first, second)]
                pl.when(jnp.logical_not(swap))(copies[0].start)
                pl.when(swap)(copies[1].start)
                sent.append(copies[0])

            r.update(need=need, keep=keep, keep_either=keep_either, core=core_ref[0])
            body(len_ref, r)
            need(*list(waiting))
            for copy in sent:
                copy.wait()

        def idle():
            for copy in everywhere:
                copy.wait()

        pl.when(active)(run)
        if fetched:
            pl.when(jnp.logical_not(active))(idle)

    def pinned(array):
        return pltpu.with_memory_space_constraint(array, pltpu.HBM)

    results = pl.pallas_call(
        kernel,
        out_shape=[pltpu.HBM(a.shape, a.dtype) for a, _ in stores.values()] + list(outs.values()),
        in_specs=[smem] * 3 + [vmem] * len(ins) + [hbm] * (len(loads) + len(vectors) + len(fetched) + len(aliases)),
        out_specs=[hbm] * len(stores) + [vmem] * len(outs),
        scratch_shapes=list(places.values()) + [pltpu.SemaphoreType.DMA((64,))],
        input_output_aliases={3 + len(in_names) + k: out_names.index(n) for k, n in enumerate(aliases)},
        compiler_params=pltpu.CompilerParams(vmem_limit_bytes=vmem_mib * 1024 * 1024),
        cost_estimate=pl.CostEstimate(flops=int(us * 1.15e9), bytes_accessed=0, transcendentals=0),
        name=name,
    )(
        section,
        core,
        lengths,
        *ins.values(),
        *[pinned(a) for a, _ in loads.values()],
        *[pinned(a) for a in vectors.values()],
        *[pinned(a) for a in fetched.values()],
        *[pinned(a) for a in aliases.values()],
    )
    return Refs(zip(out_names, results))


def exchange(block, axis, bit):
    n = lax.axis_size(axis)
    return lax.ppermute(block, axis, [(i, i ^ (1 << bit)) for i in range(n)])


def shifted(block, axis, distance):
    devices = range(lax.axis_size(axis))
    route = [(i - distance, i) for i in devices if i - distance in devices]
    return lax.ppermute(block, axis, route)


def reduce_step(block, bit, index):
    half = block.shape[0] // 2
    side = (index >> bit) & 1
    away = lax.dynamic_slice_in_dim(block, (1 - side) * half, half, 0)
    kept = lax.dynamic_slice_in_dim(block, side * half, half, 0)
    return (kept.astype(f32) + exchange(away, "dp", bit).astype(f32)).astype(bf16)


def gather_step(block, bit, index):
    side = (index >> bit) & 1
    other = exchange(block, "dp", bit)
    return jnp.where(side == 0, jnp.concatenate([block, other]), jnp.concatenate([other, block]))


class Summing:
    def __init__(self, cuts):
        self.cuts = cuts
        self.index = lax.axis_index("dp")
        self.bits = lax.axis_size("dp").bit_length() - 1
        self.orders = [list(range(1, self.bits)) for _ in cuts]
        if self.bits > 2:
            for order in self.orders[1:]:
                order[0], order[1] = order[1], order[0]

    def begin(self, kept, away):
        mine = (kept.astype(f32) + exchange(away, "dp", 0).astype(f32)).astype(bf16)
        self.parts = [mine[low:high] for low, high in zip((0, *self.cuts), self.cuts)]

    def reduce(self, step):
        self.parts = [reduce_step(p, o[step], self.index) for p, o in zip(self.parts, self.orders)]

    def gather(self, step):
        self.parts = [gather_step(p, o[step], self.index) for p, o in zip(self.parts, self.orders)]

    def wait(self, *others):
        self.parts = list(after(self.parts, *others))

    def end(self):
        return self.parts, [exchange(part, "dp", 0) for part in self.parts]


def after(arrays, *others):
    return lax.optimization_barrier((tuple(arrays), others))[0]


def put_together(name, write, core, halves, shapes, us):
    mine, other = halves
    bounds = [0]
    for part in mine:
        bounds.append(bounds[-1] + part.shape[0])
    count = 2 * len(mine)
    large = [k for k, shape in enumerate(shapes) if len(shape) == 3]

    def kernel(core_ref, *refs):
        sources, results = refs[:count], refs[count : count + len(shapes)]
        own, outs = refs[count + len(shapes) :][:count], list(results)
        for place, k in enumerate(large):
            outs[k] = refs[2 * count + len(shapes) + place]
        sems = refs[-1]
        loads = [pltpu.make_async_copy(source, target, sems.at[k]) for k, (source, target) in enumerate(zip(sources, own))]
        for copy in loads:
            copy.start()

        def rows(high_half):
            mine_here = core_ref[0] == (1 if high_half else 0)

            def get(first, last):
                pieces = []
                for k, (low, high) in enumerate(zip(bounds, bounds[1:])):
                    if first < high and last > low:
                        part = slice(max(first, low) - low, min(last, high) - low)
                        pieces.append(jnp.where(mine_here, own[k][part, :], own[len(mine) + k][part, :]).astype(f32))
                return pieces[0] if len(pieces) == 1 else jnp.concatenate(pieces)

            return get

        for copy in loads:
            copy.wait()
        sent = []

        def send(k):
            copy = pltpu.make_async_copy(outs[k], results[k], sems.at[count + k])
            copy.start()
            sent.append(copy)

        write(rows(False), rows(True), outs, send)
        for copy in sent:
            copy.wait()

    vmem = pl.BlockSpec(memory_space=pltpu.VMEM)
    hbm = pl.BlockSpec(memory_space=pltpu.HBM)
    pinned = [pltpu.with_memory_space_constraint(part, pltpu.HBM) for part in (*mine, *other)]
    return pl.pallas_call(
        kernel,
        out_shape=[pltpu.HBM(s, f32) if k in large else jax.ShapeDtypeStruct(s, f32) for k, s in enumerate(shapes)],
        in_specs=[pl.BlockSpec(memory_space=pltpu.SMEM)] + [hbm] * count,
        out_specs=[hbm if k in large else vmem for k in range(len(shapes))],
        scratch_shapes=[pltpu.VMEM(part.shape, bf16) for part in pinned]
        + [pltpu.VMEM(shapes[k], f32) for k in large]
        + [pltpu.SemaphoreType.DMA((count + len(shapes),))],
        compiler_params=pltpu.CompilerParams(vmem_limit_bytes=20 * 1024 * 1024),
        cost_estimate=pl.CostEstimate(flops=int(us * 1.15e9), bytes_accessed=0, transcendentals=0),
        name=name,
    )(core, *pinned)


def write_ffn(low, high, outs, send):
    inner, outer, wo = outs
    for j in range(COLS):
        inner[0, :, j * D : (j + 1) * D] = low(j * D, (j + 1) * D)
    send(0)
    for j in range(COLS):
        outer[0, j * D : (j + 1) * D, :] = high(j * D, (j + 1) * D)
    send(1)
    wo[0, 0 : D // 2] = low(OA, W2)
    wo[0, D // 2 : D] = high(OA, W2)
    send(2)


def write_attention(low, high, outs, send):
    wq, wk, wv, bq, bk, bv, bo, g1, s1, c1, c2, g2, s2 = outs
    wq[0] = low(AQ, VA)
    wk[0] = high(AQ, VA)
    wv[0, 0 : D // 2] = low(VA, ASMALL)
    wv[0, D // 2 : D] = high(VA, ASMALL)
    for k in range(3):
        send(k)
    small = low(ASMALL, ASMALL + SMALL)
    for ref, row in ((bq, QB), (bk, KB), (bv, VB), (bo, OB), (g1, G1), (s1, S1), (c2, C2), (g2, G2), (s2, S2)):
        ref[...] = small[row : row + 1, :]
    for j in range(COLS):
        c1[:, j * D : (j + 1) * D] = small[C1 + j : C1 + j + 1, :]


FFN_SHAPES = [(1, D, FF), (1, FF, D), (1, D, D)]
ATT_SHAPES = [(1, D, D)] * 3 + [(1, D)] * 6 + [(1, FF)] + [(1, D)] * 3


def local(tokens, cotangent, lengths, *weights):
    section = lax.axis_index("section").astype(jnp.int32).reshape(1)
    core = (lax.axis_index("dp") & 1).astype(jnp.int32).reshape(1)
    cos, sin = rotary_constants()
    w = dict(zip(WNAMES, (m[0] if m.ndim == 3 else m for m in weights)))
    call = functools.partial(kernel_call, section=section, core=core, lengths=lengths)
    rows_out = jax.ShapeDtypeStruct(tokens.shape, bf16)
    rows_outf = jax.ShapeDtypeStruct(tokens.shape, f32)
    ffn_shape = jax.ShapeDtypeStruct((FROWS, D), bf16)
    ffn_half = jax.ShapeDtypeStruct((FROWS // 2, D), bf16)
    att_shape = jax.ShapeDtypeStruct((AROWS, D), bf16)
    att_half = jax.ShapeDtypeStruct((AROWS // 2, D), bf16)
    held = {n: w[n] for n in ("wq", "wk", "wv", "wo", "w1", "w2")}
    held = dict(wq=held.pop("wq"), cos=jnp.asarray(cos), sin=jnp.asarray(sin), **held)

    def first_forward(block, held, fetch, before):
        def body(len_ref, r):
            forward(r, read_ends(len_ref, block), r.h, F_COMPACT[block])
            r.keep("rows", source=r.h)

        return call(
            body,
            0,
            f"first_forward_{block}",
            loads=dict(x=(tokens, block)),
            ins={} if fetch else held,
            fetched=held if fetch else {},
            vectors={n: w[n] for n in LINES} if fetch else {},
            stores=dict(**STATE, rows=(rows_out, block)),
            outs=dict(h=ROW),
            scratch=dict(stats=SCALES, total=ROWF),
            aliases=before,
            us=10,
        )

    f0 = first_forward(0, held, True, None)
    held = {n: f0[n] for n in ("lines", *held)}
    x0 = shifted(f0.h, "section", 1)
    f1 = first_forward(1, held, False, dict(rows=f0.rows))
    x1 = shifted(f1.h, "section", 1)

    kept = ("cb", "ub", "gb", "df", "dz", "da", "dq", "dk", "dv")
    every = dict(**STATE, **STEP)

    def second_layer(block, x, before):
        def body(len_ref, r):
            ends = read_ends(len_ref, block)
            forward(r, ends, r.rows)
            r.keep("rows")
            r.need("cotangent")
            ffn_back(r.cotangent[...], r, ends)
            attention_back(r, ends, compact=B_COMPACT[block])
            r.keep("sm")

        return call(
            body,
            1,
            f"second_layer_{block}",
            loads=dict(cotangent=(cotangent, block)),
            ins=dict(x=x, **held),
            stores=dict(rows=(rows_out, block), dh=(rows_outf, block), sm=SMALLS, **{n: every[n] for n in kept}),
            outs=dict(dhb=ROW),
            scratch=dict(stats=SCALES, total=ROWF, **{n: every[n] for n in every if n not in kept}),
            aliases=before,
            us=20,
        )

    s0 = second_layer(0, x0, dict(rows=f1.rows))
    g0 = shifted(s0.dhb, "section", -1)
    s1 = second_layer(1, x1, dict(rows=s0.rows, dh=s0.dh))
    g1 = shifted(s1.dhb, "section", -1)

    def both(names):
        return {n + str(b): s[n] for b, s in enumerate((s0, s1)) for n in names}

    ffn_names = ("ub", "dz", "gb", "df", "cb", "da")
    att_names = ("x", "dq", "dk", "dv")

    def second_ffn(len_ref, r):
        ffn_terms(r, [[n + str(b) for n in ffn_names] for b in range(MICRO)], None, r.ffn, True)

    ffn = call(
        second_ffn,
        1,
        "second_ffn",
        loads=both(("ub", "dz", "cb", "da", "gb", "df")),
        stores=dict(kept=ffn_half, away=ffn_half),
        scratch=dict(turned=TURNED[2], ffn=ffn_shape),
    )

    def second_attention(len_ref, r):
        attention_terms(r, [[n + str(b) for n in att_names] for b in range(MICRO)], ("sm0", "sm1"), None, r.att, True)

    att = call(
        second_attention,
        1,
        "second_attention",
        loads=both(("dv", "dq", "sm", "dk")),
        ins=dict(x0=x0, x1=x1),
        stores=dict(kept=att_half, away=att_half),
        scratch=dict(att=att_shape),
    )

    def first_backward_0(len_ref, r):
        ends = read_ends(len_ref, 0)
        ffn_back(r.grad[...].astype(f32), r, ends)
        ffn_terms(r, [ffn_names], None, r.ffn)
        r.keep("ffn")
        attention_back(r, ends)
        r.keep("sm")
        attention_terms(r, [att_names], None, None, r.att)
        r.keep("att")

    order = ("n2", "scales", "gp", "n1", "ub", "cb", "gb", "qb", "kb", "vb", "lse")
    b0 = call(
        first_backward_0,
        0,
        "first_backward_0",
        loads=dict(**{n: f0[n] for n in order}, x=(tokens, 0)),
        ins=dict(grad=g0, **held),
        stores=dict(
            dh=(rows_outf, 0),
            sm=SMALLS,
            ffn=jax.ShapeDtypeStruct((FROWS, D), f32),
            att=jax.ShapeDtypeStruct((AROWS, D), f32),
        ),
        scratch=dict(stats=SCALES, total=ROWF, turned=TURNED[1], **STEP),
        aliases=dict(dh=s1.dh),
        us=18,
    )

    def first_ffn_1(len_ref, r):
        ffn_back(r.grad[...].astype(f32), r, read_ends(len_ref, 1))
        r.need("start")
        ffn_terms(r, [ffn_names], r.start, r.ffn, True)

    b1 = call(
        first_ffn_1,
        0,
        "first_ffn_1",
        loads=dict(**{n: f1[n] for n in order[:7]}, start=b0.ffn),
        ins=dict(grad=g1, lines=held["lines"], w1=held["w1"], w2=held["w2"]),
        stores=dict(kept=ffn_half, away=ffn_half),
        outs=dict(ds1=ROWF, da=ROW, sm=SMALLS),
        scratch=dict(stats=SCALES, total=ROWF, turned=TURNED[1], df=ROW, dz=WIDE, ffn=ffn_shape),
        aliases=dict(kept=ffn.kept, away=ffn.away),
        us=8,
    )

    def first_attention_1a(len_ref, r):
        attention_back(r, read_ends(len_ref, 1), (0,))
        for n in ("dq", "dk", "dv"):
            r[n + "0"][...] = r[n][:, 0:128]

    strip = jax.ShapeDtypeStruct((SEQ_LEN, 128), bf16)
    b2 = call(
        first_attention_1a,
        0,
        "first_attention_1a",
        loads={n: f1[n] for n in order[7:]},
        ins=dict(da=b1.da, **{n: held[n] for n in ("cos", "sin", "wo")}),
        outs=dict(dc=ROW, dq0=strip, dk0=strip, dv0=strip),
        scratch=dict(dq=ROW, dk=ROW, dv=ROW),
        us=4,
    )

    def first_attention_1b(len_ref, r):
        r.sm[...] = r.sm_in[...]
        for n in ("dq", "dk", "dv"):
            r[n][:, 0:128] = r[n + "0"][...]
        attention_back(r, read_ends(len_ref, 1), (1, 2))
        r.need("start")
        attention_terms(r, [att_names], ("sm", "sm0"), r.start, r.att, True)

    early, late = Summing(FCUTS), Summing(ACUTS)
    last = early.bits - 2
    early.begin(b1.kept, b1.away)
    b2, early.parts = after((dict(b2), early.parts), b2.dc)
    b3 = call(
        first_attention_1b,
        0,
        "first_attention_1b",
        loads=dict(**{n: f1[n] for n in order[7:]}, x=(tokens, 1), sm0=b0.sm, start=b0.att),
        ins=dict(ds1=b1.ds1, sm_in=b1.sm, **b2, **{n: held[n] for n in ("cos", "sin", "wq", "wk", "wv")}),
        stores=dict(kept=att_half, away=att_half, dh=(rows_outf, 1)),
        scratch=dict(dq=ROW, dk=ROW, dv=ROW, sm=SMALLS, att=att_shape),
        aliases=dict(kept=att.kept, away=att.away, dh=b0.dh),
        us=10,
    )
    early.reduce(0)
    kept, away, *early.parts = after((b3.kept, b3.away, *early.parts))
    late.begin(kept, away)
    plan = [(early.reduce, step) for step in range(1, last + 1)] + [(early.gather, last - step) for step in range(last + 1)]
    chase = [(late.reduce, step) for step in range(last + 1)] + [(late.gather, last - step) for step in range(last + 1)]
    for (lead, step), (follow, behind) in zip(plan, [(None, 0)] + chase):
        if follow is not None:
            follow(behind)
        lead(step)
        if follow is None:
            late.wait(*early.parts)
            early.wait(*late.parts)
        else:
            both_parts = after((*late.parts, *early.parts))
            late.parts, early.parts = list(both_parts[: len(late.parts)]), list(both_parts[len(late.parts) :])
    ends = early.end()
    for follow, behind in chase[len(plan) - 1 :]:
        follow(behind)
    late_ends = late.end()
    inner, outer, wo = put_together("ffn_gradients", write_ffn, core, ends, FFN_SHAPES, 5)
    late_ends = after(late_ends, wo)
    (wq, wk, wv, bq, bk, bv, bo, g1_, s1_, c1, c2, g2, s2) = put_together(
        "attention_gradients", write_attention, core, late_ends, ATT_SHAPES, 3
    )
    return (
        s1.rows[None],
        b3.dh[None],
        wq,
        bq,
        wk,
        bk,
        wv,
        bv,
        wo,
        bo,
        g1_,
        s1_,
        inner,
        c1,
        outer,
        c2,
        g2,
        s2,
    )


def solution(mesh):
    square, line = P("section", None, None), P("section", None)
    weights = (square, line) * 4 + (line, line) + (square, line) * 2 + (line, line)
    rows = P("section", "dp", None)
    return jax.shard_map(
        local,
        mesh=mesh,
        in_specs=(P("dp", None),) * 3 + weights,
        out_specs=(rows, rows) + weights,
        check_vma=False,
    )
```

```python
import functools
import itertools
import math

import jax
import jax.numpy as jnp
import numpy as np
from jax import lax
from jax.experimental import pallas as pl
from jax.experimental.pallas import tpu as pltpu
from jax.sharding import PartitionSpec as P

D = 384
HEADS = 6
HEAD_DIM = 64
FF = 1536
SEQ_LEN = 512
MICRO = 2
COLS = FF // D

norm_eps = 1e-12
rope_base = 10000.0
far = -1e9

bf16 = jnp.bfloat16
f32 = jnp.float32

NT = (((1,), (1,)), ((), ()))
TN = (((0,), (0,)), ((), ()))

QB, KB, VB, OB, G1, S1, C1, C2, G2, S2 = 0, 1, 2, 3, 4, 5, 6, 10, 11, 12
SMALL = 16
W1, OA, W2, OB2 = 0, 1536, 1728, 3264
FROWS, FCUTS = 3456, (896, 1728)
AQ, VA, ASMALL, AK, VB2 = 0, 384, 576, 640, 1024
AROWS, ACUTS = 1280, (640,)


def rotary_constants():
    places = np.arange(SEQ_LEN, dtype=np.float64)[:, None]
    pairs = (np.arange(128) // 2) % (HEAD_DIM // 2)
    angles = places * np.exp(pairs * (-2.0 * math.log(rope_base) / HEAD_DIM))[None, :]
    sign = np.where(np.arange(128) % 2 == 0, -1.0, 1.0)[None, :]
    return np.cos(angles).astype(np.float32), (np.sin(angles) * sign).astype(np.float32)


def dot(a, b):
    return jnp.dot(a, b, preferred_element_type=f32)


def dot_nt(a, b):
    return lax.dot_general(a, b, NT, preferred_element_type=f32)


def dot_tn(a, b):
    return lax.dot_general(a, b, TN, preferred_element_type=f32)


def segments(ends, places):
    return sum((places >= e).astype(jnp.int32) for e in ends)


def lane_iota(width=128):
    return lax.broadcasted_iota(jnp.int32, (SEQ_LEN, width), 1)


def turn(values, cos, sin):
    lane = lane_iota()
    parts = []
    for j in range(D // 128):
        u = values[:, j * 128 : (j + 1) * 128]
        partner = jnp.where(lane % 2 == 0, pltpu.roll(u, 127, 1), pltpu.roll(u, 1, 1))
        parts.append(u * cos + partner * sin)
    return jnp.concatenate(parts, axis=1)


def normalize(summed):
    centered = summed - jnp.mean(summed, axis=-1, keepdims=True)
    scale = lax.rsqrt(jnp.mean(centered * centered, axis=-1, keepdims=True) + norm_eps)
    return centered * scale, scale


def normalize_back(grad, normed, scale):
    return scale * (
        grad
        - jnp.mean(grad, axis=-1, keepdims=True)
        - normed * jnp.mean(grad * normed, axis=-1, keepdims=True)
    )


def marks(ends):
    lane = lane_iota() % HEAD_DIM
    rows = lax.broadcasted_iota(jnp.int32, (SEQ_LEN, 1), 0)
    own = lane == segments(ends, rows)
    query_marks = own.astype(f32).astype(bf16)
    key_marks = jnp.where(own | (lane > 4), 0.0, far).astype(bf16)
    return query_marks, key_marks


class Refs(dict):
    __getattr__ = dict.__getitem__


def read_ends(len_ref, block):
    ends, total = [], 0
    for j in range(4):
        total = total + len_ref[block, j]
        ends.append(total)
    return ends


def live_rows(ends):
    rows = lax.broadcasted_iota(jnp.int32, (SEQ_LEN, 1), 0)
    return (rows < ends[3]).astype(f32)


def lanes(index, width):
    if isinstance(index, int):
        return slice(index * width, (index + 1) * width)
    return pl.ds(pl.multiple_of(index * width, width), width)


F_COMPACT = (False, True)
B_COMPACT = (True, True)


def repeat(steps, step, compact):
    if compact:

        def body(j, carry):
            step(j)
            return carry

        lax.fori_loop(steps[0], steps[-1] + 1, body, 0)
    else:
        for j in steps:
            step(j)


def line(r, name):
    row = LINES[name]
    return r.lines[row : row + 1, :]


def forward(r, ends, h_ref, compact=False):
    r.need("x", "lines", "wq", "cos", "sin")
    x, cos, sin = r.x[...], r.cos[...], r.sin[...]
    r.qb[...] = turn(dot(x, r.wq[...]) + line(r, "bq"), cos, sin).astype(bf16)
    r.need("wk")
    r.kb[...] = turn(dot(x, r.wk[...]) + line(r, "bk"), cos, sin).astype(bf16)
    r.need("wv")
    r.vb[...] = (dot(x, r.wv[...]) + line(r, "bv")).astype(bf16)
    r.keep("qb", "kb", "vb")
    query_marks, key_marks = marks(ends)

    def attend(pair):
        lane = lane_iota()
        zero = jnp.zeros((SEQ_LEN, 128), bf16)
        one = jnp.ones((SEQ_LEN, 128), bf16)
        cols = lanes(pair, 128)
        q2, k2, v2 = r.qb[:, cols] * jnp.asarray(HEAD_DIM**-0.5, bf16), r.kb[:, cols], r.vb[:, cols]
        raised, tops, weighted = [], [], []
        for side in range(2):
            mine = (lane >= HEAD_DIM) == (side == 1)
            scores = dot_nt(jnp.where(mine, q2, query_marks), jnp.where(mine, k2, key_marks))
            top = jnp.max(scores, axis=-1, keepdims=True)
            raised.append(jnp.exp(scores - top).astype(bf16))
            tops.append(top)
            weighted.append(jnp.concatenate([jnp.where(mine, v2, zero), jnp.where(mine, one, zero)], axis=1))
        both = dot(jnp.concatenate(raised, axis=1), jnp.concatenate(weighted, axis=0))
        total = both[:, 128:]
        r.cb[:, cols] = (both[:, :128] / total).astype(bf16)
        log_total = jnp.log(total)
        for side in range(2):
            value = tops[side] + log_total[:, side * HEAD_DIM : side * HEAD_DIM + 1]
            r.stats[...] = jnp.where(lane == 2 * pair + side, value, r.stats[...])

    repeat(range(HEADS // 2), attend, compact)
    r.lse[...] = r.stats[...].T[:8]
    r.keep("cb", "lse")
    r.need("wo")
    attended = dot(r.cb[...], r.wo[...]) + line(r, "bo")
    n1, r1 = normalize(x.astype(f32) + attended)
    r.n1[...] = n1
    u1 = n1 * line(r, "g1") + line(r, "s1")
    r.ub[...] = u1.astype(bf16)
    r.keep("n1", "ub")
    r.total[...] = u1 + line(r, "c2")
    r.need("w1", "w2")

    def widen(j):
        cols = lanes(j, D)
        z = dot(r.ub[...], r.w1[:, cols]) + r.lines[pl.ds(LINES["c1"] + j, 1), :]
        below = 0.5 + 0.5 * lax.erf(z * 0.7071067811865476)
        gb = (z * below).astype(bf16)
        r.gb[:, cols] = gb
        r.gp[:, cols] = (below + z * (jnp.exp(-0.5 * z * z) * 0.3989422804014327)).astype(bf16)
        if not compact:
            r.keep("gb", "gp", cols=cols)
        r.total[...] += dot(gb, r.w2[lanes(j, D), :])

    repeat(range(COLS), widen, compact)
    if compact:
        r.keep("gb", "gp")
    n2, r2 = normalize(r.total[...])
    r.n2[...] = n2
    lane = lane_iota()
    r.scales[...] = jnp.where(lane == 0, r1, r2)
    h_ref[...] = ((n2 * line(r, "g2") + line(r, "s2")) * live_rows(ends)).astype(bf16)
    r.keep("n2", "scales")


def column_sum(values):
    return jnp.sum(values, axis=0, keepdims=True)


def ffn_back(grad, r, ends, compact=False):
    grad = grad * live_rows(ends)
    r.need("n2", "scales", "lines")
    n2 = r.n2[...]
    r.sm[G2 : G2 + 1, :] = column_sum(grad * n2)
    r.sm[S2 : S2 + 1, :] = column_sum(grad)
    ds2 = normalize_back(grad * line(r, "g2"), n2, r.scales[:, 1:2])
    df = ds2.astype(bf16)
    r.df[...] = df
    r.sm[C2 : C2 + 1, :] = column_sum(df.astype(f32))
    r.total[...] = ds2
    r.keep("df")
    r.need("w1", "w2", "gp")

    def narrow(j):
        cols = lanes(j, D)
        dz = (dot_nt(r.df[...], r.w2[lanes(j, D), :]) * r.gp[:, cols].astype(f32)).astype(bf16)
        r.dz[:, cols] = dz
        if not compact:
            r.keep("dz", cols=cols)
        r.sm[pl.ds(C1 + j, 1), :] = column_sum(dz.astype(f32))
        r.total[...] += dot_nt(dz, r.w1[:, cols])

    repeat(range(COLS), narrow, compact)
    if compact:
        r.keep("dz")
    r.need("n1")
    du1, n1 = r.total[...], r.n1[...]
    r.sm[G1 : G1 + 1, :] = column_sum(du1 * n1)
    r.sm[S1 : S1 + 1, :] = column_sum(du1)
    ds1 = normalize_back(du1 * line(r, "g1"), n1, r.scales[:, 0:1])
    r.ds1[...] = ds1
    da = ds1.astype(bf16)
    r.da[...] = da
    r.sm[OB : OB + 1, :] = column_sum(da.astype(f32))
    r.keep("da", "ds1")


def attention_back(r, ends, pairs=(0, 1, 2), compact=False):
    if 0 in pairs:
        r.need("da", "wo")
        r.dc[...] = dot_nt(r.da[...], r.wo[...]).astype(bf16)
    query_marks, key_marks = marks(ends)
    r.need("qb", "kb", "vb", "lse", "cos", "sin")

    def attend(pair):
        lane = lane_iota()
        first = lane < HEAD_DIM
        zero = jnp.zeros((SEQ_LEN, 128), bf16)
        scale = jnp.asarray(HEAD_DIM**-0.5, bf16)
        cos, sin = r.cos[...], r.sin[...]
        cols = lanes(pair, 128)
        q2, k2, v2, dc2 = r.qb[:, cols] * scale, r.kb[:, cols], r.vb[:, cols], r.dc[:, cols]
        grads, dks, dvs = [], [], []
        for side in range(2):
            head = 2 * pair + side
            mine = (lane >= HEAD_DIM) == (side == 1)
            scores = dot_nt(jnp.where(mine, k2, key_marks), jnp.where(mine, q2, query_marks))
            shares = jnp.exp(scores - r.lse[pl.ds(head, 1), :])
            grad_shares = dot_nt(jnp.where(mine, v2, zero), dc2)
            row = jnp.sum(shares * grad_shares, axis=0, keepdims=True)
            grad_scores = (shares * (grad_shares - row)).astype(bf16)
            grads.append(grad_scores)
            dvs.append(dot(shares.astype(bf16), dc2))
            dks.append(dot(grad_scores, q2))
        k2s = k2 * scale
        keys = jnp.concatenate([jnp.where(first, k2s, zero), jnp.where(first, zero, k2s)], axis=0)
        dq = dot(keys.T, jnp.concatenate(grads, axis=0)).T
        dk = jnp.where(first, dks[0], dks[1])

        def back(u):
            partner = jnp.where(lane % 2 == 0, pltpu.roll(u, 127, 1), pltpu.roll(u, 1, 1))
            return (u * cos - partner * sin).astype(bf16)

        r.dq[:, cols] = back(dq)
        r.dk[:, cols] = back(dk)
        r.dv[:, cols] = jnp.where(first, dvs[0], dvs[1]).astype(bf16)
        if not compact:
            r.keep("dq", "dk", "dv", cols=cols)

    repeat(pairs, attend, compact)
    if HEADS // 2 - 1 not in pairs:
        return
    if compact:
        r.keep("dq", "dk", "dv")
    dq, dk, dv = r.dq[...], r.dk[...], r.dv[...]
    r.need("ds1", "wq", "wk", "wv")
    dh = r.ds1[...] + dot_nt(dq, r.wq[...]) + dot_nt(dk, r.wk[...]) + dot_nt(dv, r.wv[...])
    r.dh[...] = dh
    r.keep("dh")
    if "dhb" in r:
        r.dhb[...] = dh.astype(bf16)
    r.sm[QB : QB + 1, :] = column_sum(dq.astype(f32))
    r.sm[KB : KB + 1, :] = column_sum(dk.astype(f32))
    r.sm[VB : VB + 1, :] = column_sum(dv.astype(f32))


def add_up(total, start, put, *places):
    for row, first, last in places:
        value = total[first:last]
        if start is not None:
            value = value + start[row : row + last - first, :]
        put(row, value)


def into(ref):
    def put(row, value):
        ref[row : row + value.shape[0], :] = value.astype(ref.dtype)

    return put


def ffn_terms(r, sets, start, put, done=None):
    for k, (ub, dz, gb, df, cb, da) in enumerate(sets):
        r.need(ub, dz, cb, da)
        r.turned[k] = r[ub][...].T
    total = sum(dot_tn(r[s[4]][...], r[s[5]][...]) for s in sets)
    add_up(total, start, put, (OA, 0, D // 2), (OB2, D // 2, D))
    for j in range(COLS):
        cols = lanes(j, D)
        total = sum(dot(r.turned[k], r[s[1]][:, cols]) for k, s in enumerate(sets))
        add_up(total, start, put, (W1 + j * D, 0, D))
    if done:
        done(0)
    for s in sets:
        r.need(s[2], s[3])
    for j in range(COLS):
        cols = lanes(j, D)
        total = sum(dot_tn(r[s[2]][:, cols], r[s[3]][...]) for s in sets)
        add_up(total, start, put, (W2 + j * D, 0, D))
    if done:
        done(1)


def attention_terms(r, sets, smalls, start, put, done=None):
    for names in sets:
        r.need(*names)

    def total(right):
        return sum(dot_tn(r[s[0]][...], r[s[right]][...]) for s in sets)

    add_up(total(3), start, put, (VA, 0, D // 2), (VB2, D // 2, D))
    add_up(total(1), start, put, (AQ, 0, D))
    if smalls:
        r.need(*smalls)
        values = sum(r[n][...] for n in smalls)
        rest = jnp.zeros((AK - ASMALL - SMALL, D), f32)
        put(ASMALL, jnp.concatenate([values, rest]))
        put(VB2 + D // 2, jnp.zeros((AROWS - VB2 - D // 2, D), f32))
    if done:
        done(0)
    add_up(total(2), start, put, (AK, 0, D))
    if done:
        done(1)


WNAMES = ("wq", "bq", "wk", "bk", "wv", "bv", "wo", "bo", "g1", "s1", "w1", "c1", "w2", "c2", "g2", "s2")
LINES = dict(bq=0, bk=1, bv=2, bo=3, g1=4, s1=5, c1=6, c2=10, g2=11, s2=12)
ROW = jax.ShapeDtypeStruct((SEQ_LEN, D), bf16)
ROWF = jax.ShapeDtypeStruct((SEQ_LEN, D), f32)
WIDE = jax.ShapeDtypeStruct((SEQ_LEN, FF), bf16)
LSE = jax.ShapeDtypeStruct((8, SEQ_LEN), f32)
SCALES = jax.ShapeDtypeStruct((SEQ_LEN, 128), f32)
STATE = dict(qb=ROW, kb=ROW, vb=ROW, cb=ROW, lse=LSE, n1=ROWF, ub=ROW, gb=WIDE, gp=WIDE, n2=ROWF, scales=SCALES)
STEP = dict(df=ROW, dz=WIDE, ds1=ROWF, da=ROW, dc=ROW, dq=ROW, dk=ROW, dv=ROW)
SMALLS = jax.ShapeDtypeStruct((SMALL, D), f32)
TURNED = {n: jax.ShapeDtypeStruct((n, D, SEQ_LEN), bf16) for n in (1, 2)}


def kernel_call(
    bodies, name, section, core, lengths, loads=None, ins=None, fetched=None, vectors=None, stores=None, outs=None, scratch=None,
    aliases=None, vmem_mib=44, us=5
):
    loads, ins, stores, outs, scratch = (dict(d or {}) for d in (loads, ins, stores, outs, scratch))
    fetched, vectors, aliases = fetched or {}, vectors or {}, aliases or {}
    loads = {n: a if isinstance(a, tuple) else (a, None) for n, a in loads.items()}
    stores = {n: a if isinstance(a, tuple) else (a, None) for n, a in stores.items()}
    outs.update({n: jax.ShapeDtypeStruct(a.shape, a.dtype) for n, a in fetched.items()})
    if vectors:
        outs["lines"] = SMALLS

    def place(shape, block):
        return pltpu.VMEM((SEQ_LEN,) + shape.shape[1:] if block is not None else shape.shape, shape.dtype)

    def part(ref, block):
        return ref if block is None else ref.at[pl.ds(block * SEQ_LEN, SEQ_LEN)]

    hbm = pl.BlockSpec(memory_space=pltpu.HBM)
    vmem = pl.BlockSpec(memory_space=pltpu.VMEM)
    smem = pl.BlockSpec(memory_space=pltpu.SMEM)
    in_names = list(ins) + list(loads) + list(vectors) + list(fetched)
    out_names = list(stores) + list(outs)
    places = {n: place(a, b) for n, (a, b) in loads.items()}
    places.update({n: place(a, b) for n, (a, b) in stores.items() if n not in (*places, "kept", "away")})
    places.update({n: pltpu.VMEM(a.shape, a.dtype) for n, a in scratch.items()})
    places.update({n: pltpu.VMEM(a.shape, a.dtype) for n, a in vectors.items()})

    def kernel(sec_ref, core_ref, len_ref, *refs):
        given = dict(zip(in_names, refs))
        rest = refs[len(in_names) + len(aliases) :]
        results = dict(zip(out_names, rest))
        own = dict(zip(places, rest[len(out_names) :]))
        sems = refs[-1]
        r = Refs(own)
        for n in ins:
            r[n] = given[n]
        for n in outs:
            r[n] = results[n]
        used = itertools.count()
        waiting = {}

        def begin(source, target):
            copy = pltpu.make_async_copy(source, target, sems.at[next(used)])
            copy.start()
            return copy

        short = [begin(given[n], own[n]) for n in vectors]
        for n in fetched:
            waiting[n] = begin(given[n], results[n])
        everywhere = list(waiting.values())
        for n, copy in zip(vectors, short):
            copy.wait()
            for j in range(vectors[n].shape[1] // D):
                r.lines[LINES[n] + j : LINES[n] + j + 1, :] = own[n][:, j * D : (j + 1) * D].astype(f32)

        def run(body, names):
            for n in names:
                waiting[n] = begin(part(given[n], loads[n][1]), own[n])
            sent = []

            def need(*names):
                for n in names:
                    if n in waiting:
                        waiting.pop(n).wait()

            def keep(*names, cols=None, source=None):
                for n in names:
                    if n in stores:
                        target, local = part(results[n], stores[n][1]), own[n] if source is None else source
                        if cols is not None:
                            target, local = target.at[:, cols], local.at[:, cols]
                        sent.append(begin(local, target))

            def share(buffer, half_rows):
                def done(half):
                    source, k = buffer.at[pl.ds(half * half_rows, half_rows)], next(used)
                    copies = [pltpu.make_async_copy(source, results[n], sems.at[k]) for n in ("kept", "away")]
                    pl.when(core_ref[0] == half)(copies[0].start)
                    pl.when(core_ref[0] != half)(copies[1].start)
                    sent.append(copies[0])

                return done

            r.update(need=need, keep=keep, share=share)
            body(len_ref, r)
            need(*list(waiting))
            for copy in sent:
                copy.wait()

        def idle():
            for copy in everywhere:
                copy.wait()

        for k in range(2):
            if k in bodies:
                body, names = bodies[k] if isinstance(bodies[k], tuple) else (bodies[k], loads)
                pl.when(sec_ref[0] == k)(functools.partial(run, body, names))
            elif fetched:
                pl.when(sec_ref[0] == k)(idle)

    def pinned(array):
        return pltpu.with_memory_space_constraint(array, pltpu.HBM)

    results = pl.pallas_call(
        kernel,
        out_shape=[pltpu.HBM(a.shape, a.dtype) for a, _ in stores.values()] + list(outs.values()),
        in_specs=[smem] * 3 + [vmem] * len(ins) + [hbm] * (len(loads) + len(vectors) + len(fetched) + len(aliases)),
        out_specs=[hbm] * len(stores) + [vmem] * len(outs),
        scratch_shapes=list(places.values()) + [pltpu.SemaphoreType.DMA((64,))],
        input_output_aliases={3 + len(in_names) + k: out_names.index(n) for k, n in enumerate(aliases)},
        compiler_params=pltpu.CompilerParams(vmem_limit_bytes=vmem_mib * 1024 * 1024),
        cost_estimate=pl.CostEstimate(flops=int(us * 1.15e9), bytes_accessed=0, transcendentals=0),
        name=name,
    )(
        section,
        core,
        lengths,
        *ins.values(),
        *[pinned(a) for a, _ in loads.values()],
        *[pinned(a) for a in vectors.values()],
        *[pinned(a) for a in fetched.values()],
        *[pinned(a) for a in aliases.values()],
    )
    return Refs(zip(out_names, results))


def flipped(block, mask):
    return lax.ppermute(block, "dp", [(i, i ^ mask) for i in range(lax.axis_size("dp"))])


def exchange(block, axis, bit):
    return flipped(block, 1 << bit)


def shifted(block, axis, distance):
    devices = range(lax.axis_size(axis))
    route = [(i - distance, i) for i in devices if i - distance in devices]
    return lax.ppermute(block, axis, route)


def reduce_step(block, bit, index):
    half = block.shape[0] // 2
    side = (index >> bit) & 1
    away = lax.dynamic_slice_in_dim(block, (1 - side) * half, half, 0)
    kept = lax.dynamic_slice_in_dim(block, side * half, half, 0)
    return (kept.astype(f32) + exchange(away, "dp", bit).astype(f32)).astype(bf16)


def gather_step(block, bit, index):
    side = (index >> bit) & 1
    other = exchange(block, "dp", bit)
    return jnp.where(side == 0, jnp.concatenate([block, other]), jnp.concatenate([other, block]))


def gather_two(block, low_bit, high_bit, index):
    both = flipped(block, (1 << low_bit) | (1 << high_bit))
    high = flipped(block, 1 << high_bit)
    low = flipped(block, 1 << low_bit)
    at_low, at_high = (index >> low_bit) & 1 == 0, (index >> high_bit) & 1 == 0

    def order(first, second, straight):
        return jnp.where(straight, jnp.concatenate([first, second]), jnp.concatenate([second, first]))

    return order(order(block, low, at_low), order(high, both, at_low), at_high)


class Summing:
    def __init__(self, cuts):
        self.cuts = cuts
        self.index = lax.axis_index("dp")
        self.bits = lax.axis_size("dp").bit_length() - 1
        self.orders = [list(range(1, self.bits)) for _ in cuts]
        if self.bits > 2:
            for order in self.orders[1:]:
                order[0], order[1] = order[1], order[0]

    def begin(self, kept, away):
        mine = (kept.astype(f32) + exchange(away, "dp", 0).astype(f32)).astype(bf16)
        self.parts = [mine[low:high] for low, high in zip((0, *self.cuts), self.cuts)]

    def reduce(self, step):
        self.parts = [reduce_step(p, o[step], self.index) for p, o in zip(self.parts, self.orders)]

    def gather(self, step):
        self.parts = [gather_step(p, o[step], self.index) for p, o in zip(self.parts, self.orders)]

    def swap(self, meanwhile=lambda: ()):
        others = [exchange(p, "dp", o[-1]) for p, o in zip(self.parts, self.orders)]
        parts = after(self.parts, *meanwhile())
        self.parts = [(p.astype(f32) + q.astype(f32)).astype(bf16) for p, q in zip(parts, others)]

    def gather_rest(self, step):
        while step > 1:
            self.gather(step)
            step -= 1
        self.parts = [
            gather_two(p, o[1], o[0], self.index) if step == 1 else p for p, o in zip(self.parts, self.orders)
        ]
        if step == 0:
            self.gather(0)

    def wait(self, *others):
        self.parts = list(after(self.parts, *others))

    def end(self):
        return self.parts, [exchange(part, "dp", 0) for part in self.parts]


def after(arrays, *others):
    return lax.optimization_barrier((tuple(arrays), others))[0]


def put_together(name, write, core, halves, shapes):
    mine, other = halves
    bounds = [0]
    for part in mine:
        bounds.append(bounds[-1] + part.shape[0])
    count = len(mine)
    large = [k for k, shape in enumerate(shapes) if len(shape) == 3]

    def kernel(core_ref, *refs):
        own, away, results = refs[:count], refs[count : 2 * count], refs[2 * count : 2 * count + len(shapes)]
        outs, sems = list(results), refs[-1]
        for place, k in zip(refs[2 * count + len(shapes) :], large):
            outs[k] = place

        def rows(half):
            mine_here = core_ref[0] == half

            def get(first, last):
                pieces = []
                for k, (low, high) in enumerate(zip(bounds, bounds[1:])):
                    if first < high and last > low:
                        part = slice(max(first, low) - low, min(last, high) - low)
                        pieces.append(jnp.where(mine_here, own[k][part, :], away[k][part, :]).astype(f32))
                return pieces[0] if len(pieces) == 1 else jnp.concatenate(pieces)

            return get

        sent = []

        def send(k, part=slice(None)):
            copy = pltpu.make_async_copy(outs[k].at[:, part], results[k].at[:, part], sems.at[len(sent)])
            copy.start()
            sent.append(copy)

        write(rows(0), rows(1), outs, send)
        for copy in sent:
            copy.wait()

    vmem = pl.BlockSpec(memory_space=pltpu.VMEM)
    hbm = pl.BlockSpec(memory_space=pltpu.HBM)
    return pl.pallas_call(
        kernel,
        out_shape=[pltpu.HBM(s, f32) if k in large else jax.ShapeDtypeStruct(s, f32) for k, s in enumerate(shapes)],
        in_specs=[pl.BlockSpec(memory_space=pltpu.SMEM)] + [vmem] * (2 * count),
        out_specs=[hbm if k in large else vmem for k in range(len(shapes))],
        scratch_shapes=[pltpu.VMEM(shapes[k], f32) for k in large] + [pltpu.SemaphoreType.DMA((16,))],
        compiler_params=pltpu.CompilerParams(vmem_limit_bytes=20 * 1024 * 1024),
        name=name,
    )(core, *mine, *other)


def write_ffn(low, high, outs, send):
    inner, outer, wo = outs
    for j in range(COLS):
        rows = slice(j * D, (j + 1) * D)
        inner[0, :, rows] = low(j * D, (j + 1) * D)
        outer[0, rows, :] = high(j * D, (j + 1) * D)
        send(1, rows)
    send(0)
    wo[0, 0 : D // 2] = low(OA, W2)
    wo[0, D // 2 : D] = high(OA, W2)
    send(2)


def write_attention(low, high, outs, send):
    wq, wk, wv, bq, bk, bv, bo, g1, s1, c1, c2, g2, s2 = outs
    wq[0] = low(AQ, VA)
    wk[0] = high(AQ, VA)
    wv[0, 0 : D // 2] = low(VA, ASMALL)
    wv[0, D // 2 : D] = high(VA, ASMALL)
    for k in range(3):
        send(k)
    small = low(ASMALL, ASMALL + SMALL)
    for ref, row in ((bq, QB), (bk, KB), (bv, VB), (bo, OB), (g1, G1), (s1, S1), (c2, C2), (g2, G2), (s2, S2)):
        ref[...] = small[row : row + 1, :]
    for j in range(COLS):
        c1[:, j * D : (j + 1) * D] = small[C1 + j : C1 + j + 1, :]


FFN_SHAPES = [(1, D, FF), (1, FF, D), (1, D, D)]
ATT_SHAPES = [(1, D, D)] * 3 + [(1, D)] * 6 + [(1, FF)] + [(1, D)] * 3


def local(tokens, cotangent, lengths, *weights):
    section = lax.axis_index("section").astype(jnp.int32).reshape(1)
    core = (lax.axis_index("dp") & 1).astype(jnp.int32).reshape(1)
    cos, sin = rotary_constants()
    w = dict(zip(WNAMES, (m[0] if m.ndim == 3 else m for m in weights)))
    call = functools.partial(kernel_call, section=section, core=core, lengths=lengths)
    rows_out = jax.ShapeDtypeStruct(tokens.shape, bf16)
    rows_outf = jax.ShapeDtypeStruct(tokens.shape, f32)
    ffn_half = jax.ShapeDtypeStruct((FROWS // 2, D), bf16)
    att_half = jax.ShapeDtypeStruct((AROWS // 2, D), bf16)
    held = {n: w[n] for n in ("wq", "wk", "wv", "wo", "w1", "w2")}
    held = dict(wq=held.pop("wq"), cos=jnp.asarray(cos), sin=jnp.asarray(sin), **held)

    def first_forward(block, held, fetch, before):
        def body(len_ref, r):
            forward(r, read_ends(len_ref, block), r.h, F_COMPACT[block])
            r.keep("rows", source=r.h)

        return call(
            {0: body},
            f"first_forward_{block}",
            loads=dict(x=(tokens, block)),
            ins={} if fetch else held,
            fetched=held if fetch else {},
            vectors={n: w[n] for n in LINES} if fetch else {},
            stores=dict(**STATE, rows=(rows_out, block)),
            outs=dict(h=ROW),
            scratch=dict(stats=SCALES, total=ROWF),
            aliases=before,
            vmem_mib=44, us=10,
        )

    f0 = first_forward(0, held, True, None)
    held = {n: f0[n] for n in ("lines", *held)}
    x0 = shifted(f0.h, "section", 1)
    f1 = first_forward(1, held, False, dict(rows=f0.rows))
    x1 = shifted(f1.h, "section", 1)

    kept = ("cb", "ub", "gb", "df", "dz", "da", "dq", "dk", "dv")
    every = dict(**STATE, **STEP)

    def second_layer(block, x, before):
        def body(len_ref, r):
            ends = read_ends(len_ref, block)
            forward(r, ends, r.rows)
            r.keep("rows")
            r.need("cotangent")
            ffn_back(r.cotangent[...], r, ends)
            attention_back(r, ends, compact=B_COMPACT[block])
            r.keep("sm")

        return call(
            {1: body},
            f"second_layer_{block}",
            loads=dict(cotangent=(cotangent, block)),
            ins=dict(x=x, **held),
            stores=dict(rows=(rows_out, block), dh=(rows_outf, block), sm=SMALLS, **{n: every[n] for n in kept}),
            outs=dict(dhb=ROW),
            scratch=dict(stats=SCALES, total=ROWF, **{n: every[n] for n in every if n not in kept}),
            aliases=before,
            vmem_mib=44, us=20,
        )

    s0 = second_layer(0, x0, dict(rows=f1.rows))
    g0 = shifted(s0.dhb, "section", -1)
    s1 = second_layer(1, x1, dict(rows=s0.rows, dh=s0.dh))
    g1 = shifted(s1.dhb, "section", -1)

    def both(names):
        return {n + str(b): s[n] for b, s in enumerate((s0, s1)) for n in names}

    ffn_names = ("ub", "dz", "gb", "df", "cb", "da")
    att_names = ("x", "dq", "dk", "dv")

    def named(names):
        return [[n + str(b) for n in names] for b in range(MICRO)]

    def first_backward_0(len_ref, r):
        ends = read_ends(len_ref, 0)
        ffn_back(r.grad[...].astype(f32), r, ends, True)
        ffn_terms(r, [ffn_names], None, into(r.ffn))
        r.keep("ffn")
        attention_back(r, ends, compact=True)
        r.keep("sm")
        attention_terms(r, [att_names], None, None, into(r.att))
        r.keep("att")

    order = ("n2", "scales", "gp", "n1", "ub", "cb", "gb", "qb", "kb", "vb", "lse")
    b0 = call(
        {0: first_backward_0},
        "first_backward_0",
        loads=dict(**{n: f0[n] for n in order}, x=(tokens, 0)),
        ins=dict(grad=g0, **held),
        stores=dict(
            dh=(rows_outf, 0),
            sm=SMALLS,
            ffn=jax.ShapeDtypeStruct((FROWS, D), f32),
            att=jax.ShapeDtypeStruct((AROWS, D), f32),
        ),
        scratch=dict(total=ROWF, turned=TURNED[1], **STEP),
        aliases=dict(dh=s1.dh),
        vmem_mib=44, us=18,
    )

    def first_ffn_1(len_ref, r):
        ffn_back(r.grad[...].astype(f32), r, read_ends(len_ref, 1))
        r.need("start")
        ffn_terms(r, [ffn_names], r.start, into(r.buffer), r.share(r.buffer, W2))

    def second_ffn(len_ref, r):
        ffn_terms(r, named(ffn_names), None, into(r.buffer), r.share(r.buffer, W2))

    mine = dict(**{n: f1[n] for n in order[:7]}, start=b0.ffn)
    theirs = both(("ub", "dz", "cb", "da", "gb", "df"))
    b1 = call(
        {0: (first_ffn_1, mine), 1: (second_ffn, theirs)},
        "ffn_terms",
        loads=dict(**mine, **theirs),
        ins=dict(grad=g1, lines=held["lines"], w1=held["w1"], w2=held["w2"]),
        stores=dict(kept=ffn_half, away=ffn_half),
        outs=dict(ds1=ROWF, da=ROW, sm=SMALLS),
        scratch=dict(buffer=jax.ShapeDtypeStruct((FROWS, D), bf16), total=ROWF, turned=TURNED[2], df=ROW, dz=WIDE),
        vmem_mib=44, us=8,
    )

    def first_attention_1a(len_ref, r):
        attention_back(r, read_ends(len_ref, 1), (0,))
        for n in ("dq", "dk", "dv"):
            r[n + "_0"][...] = r[n][:, 0:128]

    strip = jax.ShapeDtypeStruct((SEQ_LEN, 128), bf16)
    b2 = call(
        {0: first_attention_1a},
        "first_attention_1a",
        loads={n: f1[n] for n in order[7:]},
        ins=dict(da=b1.da, **{n: held[n] for n in ("cos", "sin", "wo")}),
        outs=dict(dc=ROW, dq_0=strip, dk_0=strip, dv_0=strip),
        scratch=dict(dq=ROW, dk=ROW, dv=ROW),
        vmem_mib=44, us=4,
    )

    def first_attention_1b(len_ref, r):
        r.sm[...] = r.sm_in[...]
        for n in ("dq", "dk", "dv"):
            r[n][:, 0:128] = r[n + "_0"][...]
        attention_back(r, read_ends(len_ref, 1), (1, 2))
        r.need("start")
        attention_terms(r, [att_names], ("sm", "sm_0"), r.start, into(r.buffer), r.share(r.buffer, AK))

    def second_attention(len_ref, r):
        attention_terms(r, named(att_names), ("sm0", "sm1"), None, into(r.buffer), r.share(r.buffer, AK))

    early, late = Summing(FCUTS), Summing(ACUTS)
    last = early.bits - 2
    early.begin(b1.kept, b1.away)
    b2, early.parts = after((dict(b2), early.parts), b2.dc)
    mine = dict(**{n: f1[n] for n in order[7:]}, x=(tokens, 1), sm_0=b0.sm, start=b0.att)
    theirs = both(("dv", "dq", "sm", "dk"))
    b3 = call(
        {0: (first_attention_1b, mine), 1: (second_attention, theirs)},
        "attention_terms",
        loads=dict(**mine, **theirs),
        ins=dict(
            ds1=b1.ds1, sm_in=b1.sm, x0=x0, x1=x1, **b2, **{n: held[n] for n in ("cos", "sin", "wq", "wk", "wv")}
        ),
        stores=dict(dh=(rows_outf, 1), kept=att_half, away=att_half),
        scratch=dict(buffer=jax.ShapeDtypeStruct((AROWS, D), bf16), dq=ROW, dk=ROW, dv=ROW, sm=SMALLS),
        aliases=dict(dh=b0.dh),
        vmem_mib=44, us=10,
    )
    early.reduce(0)
    kept, away, *early.parts = after((b3.kept, b3.away, *early.parts))
    late.begin(kept, away)

    def together():
        count = len(early.parts)
        parts = after((*early.parts, *late.parts))
        early.parts, late.parts = list(parts[:count]), list(parts[count:])

    for step in range(1, last):
        early.reduce(step)
    together()
    def chase():
        for step in range(last - 1):
            late.reduce(step)
        return late.parts

    early.swap(chase)
    for step in range(max(0, last - 1), last):
        late.reduce(step)
    late.swap()
    for step in reversed(range(1, last)):
        early.gather(step)
    late.gather_rest(last - 1)
    early.gather(0)
    ends = early.end()
    late_ends = late.end()
    inner, outer, wo = put_together("ffn_gradients", write_ffn, core, ends, FFN_SHAPES)
    late_ends = after(late_ends, wo)
    (wq, wk, wv, bq, bk, bv, bo, g1_, s1_, c1, c2, g2, s2) = put_together(
        "attention_gradients", write_attention, core, late_ends, ATT_SHAPES
    )
    return (
        s1.rows[None],
        b3.dh[None],
        wq,
        bq,
        wk,
        bk,
        wv,
        bv,
        wo,
        bo,
        g1_,
        s1_,
        inner,
        c1,
        outer,
        c2,
        g2,
        s2,
    )


def solution(mesh):
    square, line = P("section", None, None), P("section", None)
    weights = (square, line) * 4 + (line, line) + (square, line) * 2 + (line, line)
    rows = P("section", "dp", None)
    return jax.shard_map(
        local,
        mesh=mesh,
        in_specs=(P("dp", None),) * 3 + weights,
        out_specs=(rows, rows) + weights,
        check_vma=False,
    )
```

```python
import functools
import itertools
import math

import jax
import jax.numpy as jnp
import numpy as np
from jax import lax
from jax.experimental import pallas as pl
from jax.experimental.pallas import tpu as pltpu
from jax.sharding import PartitionSpec as P

D = 384
HEADS = 6
HEAD_DIM = 64
FF = 1536
SEQ_LEN = 512
MICRO = 2
COLS = FF // D

norm_eps = 1e-12
rope_base = 10000.0
far = -1e9

bf16 = jnp.bfloat16
f32 = jnp.float32

NT = (((1,), (1,)), ((), ()))
TN = (((0,), (0,)), ((), ()))

QB, KB, VB, OB, G1, S1, C1, C2, G2, S2 = 0, 1, 2, 3, 4, 5, 6, 10, 11, 12
SMALL = 16
W1, OA, W2, OB2 = 0, 1536, 1728, 3264
FROWS, FCUTS = 3456, (896, 1728)
AQ, VA, ASMALL, AK, VB2 = 0, 384, 576, 640, 1024
AROWS, ACUTS = 1280, (640,)


def rotary_constants():
    places = np.arange(SEQ_LEN, dtype=np.float64)[:, None]
    pairs = (np.arange(128) // 2) % (HEAD_DIM // 2)
    angles = places * np.exp(pairs * (-2.0 * math.log(rope_base) / HEAD_DIM))[None, :]
    sign = np.where(np.arange(128) % 2 == 0, -1.0, 1.0)[None, :]
    return np.cos(angles).astype(np.float32), (np.sin(angles) * sign).astype(np.float32)


def dot(a, b):
    return jnp.dot(a, b, preferred_element_type=f32)


def dot_nt(a, b):
    return lax.dot_general(a, b, NT, preferred_element_type=f32)


def dot_tn(a, b):
    return lax.dot_general(a, b, TN, preferred_element_type=f32)


def segments(ends, places):
    return sum((places >= e).astype(jnp.int32) for e in ends)


def lane_iota(width=128):
    return lax.broadcasted_iota(jnp.int32, (SEQ_LEN, width), 1)


def turn(values, cos, sin):
    lane = lane_iota()
    parts = []
    for j in range(D // 128):
        u = values[:, j * 128 : (j + 1) * 128]
        partner = jnp.where(lane % 2 == 0, pltpu.roll(u, 127, 1), pltpu.roll(u, 1, 1))
        parts.append(u * cos + partner * sin)
    return jnp.concatenate(parts, axis=1)


def normalize(summed):
    centered = summed - jnp.mean(summed, axis=-1, keepdims=True)
    scale = lax.rsqrt(jnp.mean(centered * centered, axis=-1, keepdims=True) + norm_eps)
    return centered * scale, scale


def normalize_back(grad, normed, scale):
    return scale * (
        grad
        - jnp.mean(grad, axis=-1, keepdims=True)
        - normed * jnp.mean(grad * normed, axis=-1, keepdims=True)
    )


def marks(ends):
    lane = lane_iota() % HEAD_DIM
    rows = lax.broadcasted_iota(jnp.int32, (SEQ_LEN, 1), 0)
    own = lane == segments(ends, rows)
    query_marks = own.astype(f32).astype(bf16)
    key_marks = jnp.where(own | (lane > 4), 0.0, far).astype(bf16)
    return query_marks, key_marks


class Refs(dict):
    __getattr__ = dict.__getitem__


def read_ends(len_ref, block):
    ends, total = [], 0
    for j in range(4):
        total = total + len_ref[block, j]
        ends.append(total)
    return ends


def live_rows(ends):
    rows = lax.broadcasted_iota(jnp.int32, (SEQ_LEN, 1), 0)
    return (rows < ends[3]).astype(f32)


def lanes(index, width):
    if isinstance(index, int):
        return slice(index * width, (index + 1) * width)
    return pl.ds(pl.multiple_of(index * width, width), width)


F_COMPACT = (False, True)
B_COMPACT = (True, True)


def repeat(steps, step, compact):
    if compact:

        def body(j, carry):
            step(j)
            return carry

        lax.fori_loop(steps[0], steps[-1] + 1, body, 0)
    else:
        for j in steps:
            step(j)


def line(r, name):
    row = LINES[name]
    return r.lines[row : row + 1, :]


def forward(r, ends, h_ref, compact=False):
    r.need("x", "lines", "wq", "cos", "sin")
    x, cos, sin = r.x[...], r.cos[...], r.sin[...]
    r.qb[...] = turn(dot(x, r.wq[...]) + line(r, "bq"), cos, sin).astype(bf16)
    r.need("wk")
    r.kb[...] = turn(dot(x, r.wk[...]) + line(r, "bk"), cos, sin).astype(bf16)
    r.need("wv")
    r.vb[...] = (dot(x, r.wv[...]) + line(r, "bv")).astype(bf16)
    r.keep("qb", "kb", "vb")
    query_marks, key_marks = marks(ends)

    def attend(pair):
        lane = lane_iota()
        zero = jnp.zeros((SEQ_LEN, 128), bf16)
        one = jnp.ones((SEQ_LEN, 128), bf16)
        cols = lanes(pair, 128)
        q2, k2, v2 = r.qb[:, cols] * jnp.asarray(HEAD_DIM**-0.5, bf16), r.kb[:, cols], r.vb[:, cols]
        raised, tops, weighted = [], [], []
        for side in range(2):
            mine = (lane >= HEAD_DIM) == (side == 1)
            scores = dot_nt(jnp.where(mine, q2, query_marks), jnp.where(mine, k2, key_marks))
            top = jnp.max(scores, axis=-1, keepdims=True)
            raised.append(jnp.exp(scores - top).astype(bf16))
            tops.append(top)
            weighted.append(jnp.concatenate([jnp.where(mine, v2, zero), jnp.where(mine, one, zero)], axis=1))
        both = dot(jnp.concatenate(raised, axis=1), jnp.concatenate(weighted, axis=0))
        total = both[:, 128:]
        r.cb[:, cols] = (both[:, :128] / total).astype(bf16)
        log_total = jnp.log(total)
        for side in range(2):
            value = tops[side] + log_total[:, side * HEAD_DIM : side * HEAD_DIM + 1]
            r.stats[...] = jnp.where(lane == 2 * pair + side, value, r.stats[...])

    repeat(range(HEADS // 2), attend, compact)
    r.lse[...] = r.stats[...].T[:8]
    r.keep("cb", "lse")
    r.need("wo")
    attended = dot(r.cb[...], r.wo[...]) + line(r, "bo")
    n1, r1 = normalize(x.astype(f32) + attended)
    r.n1[...] = n1
    u1 = n1 * line(r, "g1") + line(r, "s1")
    r.ub[...] = u1.astype(bf16)
    r.keep("n1", "ub")
    r.total[...] = u1 + line(r, "c2")
    r.need("w1", "w2")

    def widened(j):
        cols = lanes(j, D)
        return dot(r.ub[...], r.w1[:, cols]) + r.lines[pl.ds(LINES["c1"] + j, 1), :]

    def widen(j, z):
        cols = lanes(j, D)
        below = 0.5 + 0.5 * lax.erf(z * 0.7071067811865476)
        gb = (z * below).astype(bf16)
        r.gb[:, cols] = gb
        r.gp[:, cols] = (below + z * (jnp.exp(-0.5 * z * z) * 0.3989422804014327)).astype(bf16)
        if not compact:
            r.keep("gb", "gp", cols=cols)
        r.total[...] += dot(gb, r.w2[lanes(j, D), :])

    if compact:
        repeat(range(COLS), lambda j: widen(j, widened(j)), True)
        r.keep("gb", "gp")
    else:
        z = widened(0)
        for j in range(COLS):
            following = widened(j + 1) if j + 1 < COLS else None
            widen(j, z)
            z = following
    n2, r2 = normalize(r.total[...])
    r.n2[...] = n2
    lane = lane_iota()
    r.scales[...] = jnp.where(lane == 0, r1, r2)
    h_ref[...] = ((n2 * line(r, "g2") + line(r, "s2")) * live_rows(ends)).astype(bf16)
    r.keep("n2", "scales")


def column_sum(values):
    return jnp.sum(values, axis=0, keepdims=True)


def ffn_back(grad, r, ends, compact=False):
    grad = grad * live_rows(ends)
    r.need("n2", "scales", "lines")
    n2 = r.n2[...]
    r.sm[G2 : G2 + 1, :] = column_sum(grad * n2)
    r.sm[S2 : S2 + 1, :] = column_sum(grad)
    ds2 = normalize_back(grad * line(r, "g2"), n2, r.scales[:, 1:2])
    df = ds2.astype(bf16)
    r.df[...] = df
    r.sm[C2 : C2 + 1, :] = column_sum(df.astype(f32))
    r.total[...] = ds2
    r.keep("df")
    r.need("w1", "w2", "gp")

    def widened(j):
        return dot_nt(r.df[...], r.w2[lanes(j, D), :])

    def narrow(j, wide):
        cols = lanes(j, D)
        dz = (wide * r.gp[:, cols].astype(f32)).astype(bf16)
        r.dz[:, cols] = dz
        if not compact:
            r.keep("dz", cols=cols)
        r.sm[pl.ds(C1 + j, 1), :] = column_sum(dz.astype(f32))
        r.total[...] += dot_nt(dz, r.w1[:, cols])

    if compact:
        repeat(range(COLS), lambda j: narrow(j, widened(j)), True)
        r.keep("dz")
    else:
        wide = widened(0)
        for j in range(COLS):
            following = widened(j + 1) if j + 1 < COLS else None
            narrow(j, wide)
            wide = following
    r.need("n1")
    du1, n1 = r.total[...], r.n1[...]
    r.sm[G1 : G1 + 1, :] = column_sum(du1 * n1)
    r.sm[S1 : S1 + 1, :] = column_sum(du1)
    ds1 = normalize_back(du1 * line(r, "g1"), n1, r.scales[:, 0:1])
    r.ds1[...] = ds1
    da = ds1.astype(bf16)
    r.da[...] = da
    r.sm[OB : OB + 1, :] = column_sum(da.astype(f32))
    r.keep("da", "ds1")


def attention_back(r, ends, pairs=(0, 1, 2), compact=False):
    if 0 in pairs:
        r.need("da", "wo")
        r.dc[...] = dot_nt(r.da[...], r.wo[...]).astype(bf16)
    query_marks, key_marks = marks(ends)
    r.need("qb", "kb", "vb", "lse", "cos", "sin")

    def attend(pair):
        lane = lane_iota()
        first = lane < HEAD_DIM
        zero = jnp.zeros((SEQ_LEN, 128), bf16)
        scale = jnp.asarray(HEAD_DIM**-0.5, bf16)
        cos, sin = r.cos[...], r.sin[...]
        cols = lanes(pair, 128)
        q2, k2, v2, dc2 = r.qb[:, cols] * scale, r.kb[:, cols], r.vb[:, cols], r.dc[:, cols]
        grads, dks, dvs = [], [], []
        for side in range(2):
            head = 2 * pair + side
            mine = (lane >= HEAD_DIM) == (side == 1)
            scores = dot_nt(jnp.where(mine, k2, key_marks), jnp.where(mine, q2, query_marks))
            shares = jnp.exp(scores - r.lse[pl.ds(head, 1), :])
            grad_shares = dot_nt(jnp.where(mine, v2, zero), dc2)
            row = jnp.sum(shares * grad_shares, axis=0, keepdims=True)
            grad_scores = (shares * (grad_shares - row)).astype(bf16)
            grads.append(grad_scores)
            dvs.append(dot(shares.astype(bf16), dc2))
            dks.append(dot(grad_scores, q2))
        k2s = k2 * scale
        keys = jnp.concatenate([jnp.where(first, k2s, zero), jnp.where(first, zero, k2s)], axis=0)
        dq = dot(keys.T, jnp.concatenate(grads, axis=0)).T
        dk = jnp.where(first, dks[0], dks[1])

        def back(u):
            partner = jnp.where(lane % 2 == 0, pltpu.roll(u, 127, 1), pltpu.roll(u, 1, 1))
            return (u * cos - partner * sin).astype(bf16)

        r.dq[:, cols] = back(dq)
        r.dk[:, cols] = back(dk)
        r.dv[:, cols] = jnp.where(first, dvs[0], dvs[1]).astype(bf16)
        if not compact:
            r.keep("dq", "dk", "dv", cols=cols)

    repeat(pairs, attend, compact)
    if HEADS // 2 - 1 not in pairs:
        return
    if compact:
        r.keep("dq", "dk", "dv")
    dq, dk, dv = r.dq[...], r.dk[...], r.dv[...]
    r.sm[QB : QB + 1, :] = column_sum(dq.astype(f32))
    r.sm[KB : KB + 1, :] = column_sum(dk.astype(f32))
    r.sm[VB : VB + 1, :] = column_sum(dv.astype(f32))


def input_back(r):
    r.need("ds1", "wq", "wk", "wv")
    for rows in (pl.ds(0, SEQ_LEN // 2), pl.ds(SEQ_LEN // 2, SEQ_LEN // 2)):
        dh = r.ds1[rows, :]
        for grad, weight in ((r.dq, r.wq), (r.dk, r.wk), (r.dv, r.wv)):
            dh = dh + dot_nt(grad[rows, :], weight[...])
        r.dh[rows, :] = dh
        r.keep("dh", rows=rows)
        if "dhb" in r:
            r.dhb[rows, :] = dh.astype(bf16)


def add_up(total, start, put, *places):
    for row, first, last in places:
        value = total[first:last]
        if start is not None:
            value = value + start[row : row + last - first, :]
        put(row, value)


def into(ref):
    def put(row, value):
        ref[row : row + value.shape[0], :] = value.astype(ref.dtype)

    return put


def ffn_terms(r, sets, start, put):
    for k, (ub, dz, gb, df, cb, da) in enumerate(sets):
        r.need(ub, dz, cb, da)
        r.turned[k] = r[ub][...].T
    total = sum(dot_tn(r[s[4]][...], r[s[5]][...]) for s in sets)
    add_up(total, start, put, (OA, 0, D // 2), (OB2, D // 2, D))
    for j in range(COLS):
        cols = lanes(j, D)
        total = sum(dot(r.turned[k], r[s[1]][:, cols]) for k, s in enumerate(sets))
        add_up(total, start, put, (W1 + j * D, 0, D))
    for s in sets:
        r.need(s[2], s[3])
    for j in range(COLS):
        cols = lanes(j, D)
        total = sum(dot_tn(r[s[2]][:, cols], r[s[3]][...]) for s in sets)
        add_up(total, start, put, (W2 + j * D, 0, D))


def attention_terms(r, sets, smalls, start, put):
    for names in sets:
        r.need(*names)

    def total(right):
        return sum(dot_tn(r[s[0]][...], r[s[right]][...]) for s in sets)

    add_up(total(3), start, put, (VA, 0, D // 2), (VB2, D // 2, D))
    add_up(total(1), start, put, (AQ, 0, D))
    if smalls:
        r.need(*smalls)
        values = sum(r[n][...] for n in smalls)
        rest = jnp.zeros((AK - ASMALL - SMALL, D), f32)
        put(ASMALL, jnp.concatenate([values, rest]))
        put(VB2 + D // 2, jnp.zeros((AROWS - VB2 - D // 2, D), f32))
    add_up(total(2), start, put, (AK, 0, D))


WNAMES = ("wq", "bq", "wk", "bk", "wv", "bv", "wo", "bo", "g1", "s1", "w1", "c1", "w2", "c2", "g2", "s2")
LINES = dict(bq=0, bk=1, bv=2, bo=3, g1=4, s1=5, c1=6, c2=10, g2=11, s2=12)
ROW = jax.ShapeDtypeStruct((SEQ_LEN, D), bf16)
ROWF = jax.ShapeDtypeStruct((SEQ_LEN, D), f32)
WIDE = jax.ShapeDtypeStruct((SEQ_LEN, FF), bf16)
LSE = jax.ShapeDtypeStruct((8, SEQ_LEN), f32)
SCALES = jax.ShapeDtypeStruct((SEQ_LEN, 128), f32)
STATE = dict(qb=ROW, kb=ROW, vb=ROW, cb=ROW, lse=LSE, n1=ROWF, ub=ROW, gb=WIDE, gp=WIDE, n2=ROWF, scales=SCALES)
STEP = dict(df=ROW, dz=WIDE, ds1=ROWF, da=ROW, dc=ROW, dq=ROW, dk=ROW, dv=ROW)
SMALLS = jax.ShapeDtypeStruct((SMALL, D), f32)
TURNED = {n: jax.ShapeDtypeStruct((n, D, SEQ_LEN), bf16) for n in (1, 2)}


def kernel_call(
    bodies, name, section, core, lengths, loads=None, ins=None, fetched=None, vectors=None, through=(), stores=None, outs=None, scratch=None,
    aliases=None, vmem_mib=44, us=5
):
    loads, ins, stores, outs, scratch = (dict(d or {}) for d in (loads, ins, stores, outs, scratch))
    fetched, vectors, aliases = fetched or {}, vectors or {}, aliases or {}
    loads = {n: a if isinstance(a, tuple) else (a, None) for n, a in loads.items()}
    stores = {n: a if isinstance(a, tuple) else (a, None) for n, a in stores.items()}
    outs.update({n: jax.ShapeDtypeStruct(a.shape, a.dtype) for n, a in fetched.items()})
    if vectors:
        outs["lines"] = SMALLS
    outs.update({n: jax.ShapeDtypeStruct(loads[n][0].shape, loads[n][0].dtype) for n in through})

    unplaced = ("kept0", "away0", "kept1", "away1", "rows", "all_dh")

    def place(shape, block):
        return pltpu.VMEM((SEQ_LEN,) + shape.shape[1:] if block is not None else shape.shape, shape.dtype)

    def part(ref, block):
        return ref if block is None else ref.at[pl.ds(block * SEQ_LEN, SEQ_LEN)]

    hbm = pl.BlockSpec(memory_space=pltpu.HBM)
    vmem = pl.BlockSpec(memory_space=pltpu.VMEM)
    smem = pl.BlockSpec(memory_space=pltpu.SMEM)
    in_names = list(ins) + list(loads) + list(vectors) + list(fetched)
    out_names = list(stores) + list(outs)
    places = {n: place(a, b) for n, (a, b) in loads.items() if n not in through}
    places.update({n: place(a, b) for n, (a, b) in stores.items() if n not in (*places, *unplaced)})
    places.update({n: pltpu.VMEM(a.shape, a.dtype) for n, a in scratch.items()})
    places.update({n: pltpu.VMEM(a.shape, a.dtype) for n, a in vectors.items()})

    def kernel(sec_ref, core_ref, len_ref, *refs):
        given = dict(zip(in_names, refs))
        rest = refs[len(in_names) + len(aliases) :]
        results = dict(zip(out_names, rest))
        own = dict(zip(places, rest[len(out_names) :]))
        sems = refs[-1]
        r = Refs(own)
        for n in ins:
            r[n] = given[n]
        for n in outs:
            r[n] = results[n]
        used = itertools.count()
        waiting = {}

        def begin(source, target):
            copy = pltpu.make_async_copy(source, target, sems.at[next(used)])
            copy.start()
            return copy

        short = [begin(given[n], own[n]) for n in vectors]
        for n in fetched:
            waiting[n] = begin(given[n], results[n])
        everywhere = list(waiting.values())

        def write_lines():
            for n, copy in zip(vectors, short):
                copy.wait()
                for j in range(vectors[n].shape[1] // D):
                    r.lines[LINES[n] + j : LINES[n] + j + 1, :] = own[n][:, j * D : (j + 1) * D].astype(f32)

        def run(body, names):
            for n in names:
                waiting[n] = begin(part(given[n], loads[n][1]), r[n])
            write_lines()
            sent = []

            def need(*names):
                for n in names:
                    if n in waiting:
                        waiting.pop(n).wait()

            def keep(*names, cols=None, rows=None, source=None):
                for n in names:
                    if n in stores:
                        target, local = part(results[n], stores[n][1]), own[n] if source is None else source
                        if cols is not None:
                            target, local = target.at[:, cols], local.at[:, cols]
                        if rows is not None:
                            target, local = target.at[rows], local.at[rows] if source is None else local
                        sent.append(begin(local, target))

            def shared(buffer, cuts):
                def put(row, value):
                    buffer[row : row + value.shape[0], :] = value.astype(buffer.dtype)
                    half = row // cuts[-1]
                    for k, (low, high) in enumerate(zip((0, *cuts), cuts)):
                        first = max(row, half * cuts[-1] + low)
                        last = min(row + value.shape[0], half * cuts[-1] + high)
                        if first >= last:
                            continue
                        target, sem = pl.ds(first - half * cuts[-1] - low, last - first), sems.at[next(used)]
                        copies = [
                            pltpu.make_async_copy(buffer.at[pl.ds(first, last - first)], results[f"{n}{k}"].at[target], sem)
                            for n in ("kept", "away")
                        ]
                        pl.when(core_ref[0] == half)(copies[0].start)
                        pl.when(core_ref[0] != half)(copies[1].start)
                        sent.append(copies[0])

                return put

            r.update(need=need, keep=keep, shared=shared)
            body(len_ref, r)
            need(*list(waiting))
            for copy in sent:
                copy.wait()

        def idle():
            write_lines()
            for copy in everywhere:
                copy.wait()

        for k in range(2):
            if k in bodies:
                body, names = bodies[k] if isinstance(bodies[k], tuple) else (bodies[k], loads)
                pl.when(sec_ref[0] == k)(functools.partial(run, body, names))
            elif fetched:
                pl.when(sec_ref[0] == k)(idle)

    def pinned(array):
        return pltpu.with_memory_space_constraint(array, pltpu.HBM)

    results = pl.pallas_call(
        kernel,
        out_shape=[pltpu.HBM(a.shape, a.dtype) for a, _ in stores.values()] + list(outs.values()),
        in_specs=[smem] * 3 + [vmem] * len(ins) + [hbm] * (len(loads) + len(vectors) + len(fetched) + len(aliases)),
        out_specs=[hbm] * len(stores) + [vmem] * len(outs),
        scratch_shapes=list(places.values()) + [pltpu.SemaphoreType.DMA((64,))],
        input_output_aliases={3 + len(in_names) + k: out_names.index(n) for k, n in enumerate(aliases)},
        compiler_params=pltpu.CompilerParams(vmem_limit_bytes=vmem_mib * 1024 * 1024),
        cost_estimate=pl.CostEstimate(flops=int(us * 1.15e9), bytes_accessed=0, transcendentals=0),
        name=name,
    )(
        section,
        core,
        lengths,
        *ins.values(),
        *[pinned(a) for a, _ in loads.values()],
        *[pinned(a) for a in vectors.values()],
        *[pinned(a) for a in fetched.values()],
        *[pinned(a) for a in aliases.values()],
    )
    return Refs(zip(out_names, results))


def flipped(block, mask):
    return lax.ppermute(block, "dp", [(i, i ^ mask) for i in range(lax.axis_size("dp"))])


def exchange(block, axis, bit):
    return flipped(block, 1 << bit)


def shifted(block, axis, distance):
    devices = range(lax.axis_size(axis))
    route = [(i - distance, i) for i in devices if i - distance in devices]
    return lax.ppermute(block, axis, route)


def reduce_step(block, bit, index, others=()):
    half = block.shape[0] // 2
    side = (index >> bit) & 1
    away = lax.dynamic_slice_in_dim(block, (1 - side) * half, half, 0)
    kept = lax.dynamic_slice_in_dim(block, side * half, half, 0)
    received = exchange(away, "dp", bit)
    if others:
        kept = after((kept,), *others)[0]
    return (kept.astype(f32) + received.astype(f32)).astype(bf16)


def gather_step(block, bit, index):
    side = (index >> bit) & 1
    other = exchange(block, "dp", bit)
    return jnp.where(side == 0, jnp.concatenate([block, other]), jnp.concatenate([other, block]))


def gather_two(block, low_bit, high_bit, index):
    both = flipped(block, (1 << low_bit) | (1 << high_bit))
    high = flipped(block, 1 << high_bit)
    low = flipped(block, 1 << low_bit)
    at_low, at_high = (index >> low_bit) & 1 == 0, (index >> high_bit) & 1 == 0

    def order(first, second, straight):
        return jnp.where(straight, jnp.concatenate([first, second]), jnp.concatenate([second, first]))

    return order(order(block, low, at_low), order(high, both, at_low), at_high)


class Summing:
    def __init__(self, cuts, turned=1):
        self.cuts = cuts
        self.index = lax.axis_index("dp")
        self.bits = lax.axis_size("dp").bit_length() - 1
        self.orders = [list(range(1, self.bits)) for _ in cuts]
        if self.bits > 2:
            for order in self.orders[turned:]:
                order[0], order[1] = order[1], order[0]

    def begin(self, kept, away):
        self.parts = [
            (mine.astype(f32) + exchange(other, "dp", 0).astype(f32)).astype(bf16) for mine, other in zip(kept, away)
        ]

    def reduce(self, step, others=()):
        self.parts = [reduce_step(p, o[step], self.index, others) for p, o in zip(self.parts, self.orders)]

    def gather(self, step):
        self.parts = [gather_step(p, o[step], self.index) for p, o in zip(self.parts, self.orders)]

    def swap(self, meanwhile=lambda: ()):
        others = [exchange(p, "dp", o[-1]) for p, o in zip(self.parts, self.orders)]
        parts = after(self.parts, *meanwhile())
        self.parts = [(p.astype(f32) + q.astype(f32)).astype(bf16) for p, q in zip(parts, others)]

    def gather_rest(self, step):
        while step > 1:
            self.gather(step)
            step -= 1
        self.parts = [
            gather_two(p, o[1], o[0], self.index) if step == 1 else p for p, o in zip(self.parts, self.orders)
        ]
        if step == 0:
            self.gather(0)

    def wait(self, *others):
        self.parts = list(after(self.parts, *others))

    def end(self):
        return self.parts, [exchange(part, "dp", 0) for part in self.parts]


def after(arrays, *others):
    return lax.optimization_barrier((tuple(arrays), others))[0]


def put_together(name, write, core, halves, shapes):
    mine, other = halves
    bounds = [0]
    for part in mine:
        bounds.append(bounds[-1] + part.shape[0])
    count = len(mine)
    large = [k for k, shape in enumerate(shapes) if len(shape) == 3]

    def kernel(core_ref, *refs):
        own, away, results = refs[:count], refs[count : 2 * count], refs[2 * count : 2 * count + len(shapes)]
        outs, sems = list(results), refs[-1]
        for place, k in zip(refs[2 * count + len(shapes) :], large):
            outs[k] = place

        def rows(half):
            mine_here = core_ref[0] == half

            def get(first, last):
                pieces = []
                for k, (low, high) in enumerate(zip(bounds, bounds[1:])):
                    if first < high and last > low:
                        part = slice(max(first, low) - low, min(last, high) - low)
                        pieces.append(jnp.where(mine_here, own[k][part, :], away[k][part, :]).astype(f32))
                return pieces[0] if len(pieces) == 1 else jnp.concatenate(pieces)

            return get

        sent = []

        def send(k, part=slice(None)):
            copy = pltpu.make_async_copy(outs[k].at[:, part], results[k].at[:, part], sems.at[len(sent)])
            copy.start()
            sent.append(copy)

        write(rows(0), rows(1), outs, send)
        for copy in sent:
            copy.wait()

    vmem = pl.BlockSpec(memory_space=pltpu.VMEM)
    hbm = pl.BlockSpec(memory_space=pltpu.HBM)
    return pl.pallas_call(
        kernel,
        out_shape=[pltpu.HBM(s, f32) if k in large else jax.ShapeDtypeStruct(s, f32) for k, s in enumerate(shapes)],
        in_specs=[pl.BlockSpec(memory_space=pltpu.SMEM)] + [vmem] * (2 * count),
        out_specs=[hbm if k in large else vmem for k in range(len(shapes))],
        scratch_shapes=[pltpu.VMEM(shapes[k], f32) for k in large] + [pltpu.SemaphoreType.DMA((16,))],
        compiler_params=pltpu.CompilerParams(vmem_limit_bytes=20 * 1024 * 1024),
        name=name,
    )(core, *mine, *other)


def write_ffn(low, high, outs, send):
    inner, outer, wo = outs
    for j in range(COLS):
        rows = slice(j * D, (j + 1) * D)
        inner[0, :, rows] = low(j * D, (j + 1) * D)
        outer[0, rows, :] = high(j * D, (j + 1) * D)
        send(1, rows)
    send(0)
    wo[0, 0 : D // 2] = low(OA, W2)
    wo[0, D // 2 : D] = high(OA, W2)
    send(2)


def write_attention(low, high, outs, send):
    wq, wk, wv, bq, bk, bv, bo, g1, s1, c1, c2, g2, s2 = outs
    wq[0] = low(AQ, VA)
    wk[0] = high(AQ, VA)
    wv[0, 0 : D // 2] = low(VA, ASMALL)
    wv[0, D // 2 : D] = high(VA, ASMALL)
    for k in range(3):
        send(k)
    small = low(ASMALL, ASMALL + SMALL)
    for ref, row in ((bq, QB), (bk, KB), (bv, VB), (bo, OB), (g1, G1), (s1, S1), (c2, C2), (g2, G2), (s2, S2)):
        ref[...] = small[row : row + 1, :]
    for j in range(COLS):
        c1[:, j * D : (j + 1) * D] = small[C1 + j : C1 + j + 1, :]


FFN_SHAPES = [(1, D, FF), (1, FF, D), (1, D, D)]
ATT_SHAPES = [(1, D, D)] * 3 + [(1, D)] * 6 + [(1, FF)] + [(1, D)] * 3


def local(tokens, cotangent, lengths, *weights):
    section = lax.axis_index("section").astype(jnp.int32).reshape(1)
    core = (lax.axis_index("dp") & 1).astype(jnp.int32).reshape(1)
    cos, sin = rotary_constants()
    w = dict(zip(WNAMES, (m[0] if m.ndim == 3 else m for m in weights)))
    call = functools.partial(kernel_call, section=section, core=core, lengths=lengths)
    rows_out = jax.ShapeDtypeStruct(tokens.shape, bf16)
    rows_outf = jax.ShapeDtypeStruct(tokens.shape, f32)

    def streams(cuts):
        sizes = [high - low for low, high in zip((0, *cuts), cuts)]
        return {n + str(k): jax.ShapeDtypeStruct((m, D), bf16) for n in ("kept", "away") for k, m in enumerate(sizes)}

    held = {n: w[n] for n in ("wq", "wk", "wv", "wo", "w1", "w2")}
    held = dict(wq=held.pop("wq"), cos=jnp.asarray(cos), sin=jnp.asarray(sin), **held)

    last_state = {n: STATE[n] for n in ("n2", "scales")}

    def first_forward(block, held, fetch, left):
        def body(len_ref, r):
            for n in left:
                r.keep(n + "_0", source=r["left_" + n])
            forward(r, read_ends(len_ref, block), r.h, F_COMPACT[block])
            if not fetch:
                r.keep("rows", rows=pl.ds(0, SEQ_LEN), source=r.left_h)
                r.keep("rows", rows=pl.ds(SEQ_LEN, SEQ_LEN), source=r.h)

        return call(
            {0: body},
            f"first_forward_{block}",
            loads=dict(x=(tokens, block)),
            ins={} if fetch else dict(**held, **{"left_" + n: a for n, a in left.items()}),
            fetched=held if fetch else {},
            vectors={n: w[n] for n in LINES} if fetch else {},
            stores=dict(
                **{n: a for n, a in STATE.items() if not (fetch and n in last_state)},
                **{n + "_0": STATE[n] for n in left if n in STATE},
                **({} if fetch else dict(rows=rows_out)),
            ),
            outs=dict(h=ROW, **(last_state if fetch else {})),
            scratch=dict(stats=SCALES, total=ROWF),
            vmem_mib=44, us=10,
        )

    f0 = first_forward(0, held, True, {})
    held = {n: f0[n] for n in ("lines", *held)}
    x0 = shifted(f0.h, "section", 1)
    f1 = first_forward(1, held, False, {n: f0[n] for n in (*last_state, "h")})
    f0.update({n: f1[n + "_0"] for n in last_state})
    x1 = shifted(f1.h, "section", 1)

    kept = ("cb", "ub", "gb", "df", "dz", "da", "dq", "dk", "dv")
    every = dict(**STATE, **STEP)

    def second_layer(block, x, before, left):
        def body(len_ref, r):
            ends = read_ends(len_ref, block)
            forward(r, ends, r.h)
            r.keep("rows", source=r.h)
            r.need("cotangent")
            ffn_back(r.cotangent[...], r, ends)
            attention_back(r, ends, compact=B_COMPACT[block])
            r.keep("sm")
            input_back(r)
            if block:
                r.keep("all_dh", source=r.left_dh)

        return call(
            {1: body},
            f"second_layer_{block}",
            loads=dict(cotangent=(cotangent, block)),
            ins=dict(x=x, **held, **left),
            stores=dict(
                rows=(rows_out, block),
                sm=SMALLS,
                **{n: every[n] for n in kept},
                **(dict(all_dh=(rows_outf, 0)) if block else {}),
            ),
            outs=dict(dhb=ROW, dh=ROWF),
            scratch=dict(h=ROW, stats=SCALES, total=ROWF, **{n: every[n] for n in every if n not in kept}),
            aliases=before,
            vmem_mib=44, us=20,
        )

    s0 = second_layer(0, x0, dict(rows=f1.rows), {})
    g0 = shifted(s0.dhb, "section", -1)
    s1 = second_layer(1, x1, dict(rows=s0.rows), dict(left_dh=s0.dh))
    g1 = shifted(s1.dhb, "section", -1)

    def both(names):
        return {n + str(b): s[n] for b, s in enumerate((s0, s1)) for n in names}

    ffn_names = ("ub", "dz", "gb", "df", "cb", "da")
    att_names = ("x", "dq", "dk", "dv")

    def named(names):
        return [[n + str(b) for n in names] for b in range(MICRO)]

    def first_backward_0(len_ref, r):
        ends = read_ends(len_ref, 0)
        ffn_back(r.grad[...].astype(f32), r, ends, True)
        ffn_terms(r, [ffn_names], None, into(r.ffn))
        r.keep("ffn")
        attention_back(r, ends, compact=True)
        r.keep("sm")
        attention_terms(r, [att_names], None, None, into(r.att))
        r.keep("att")
        input_back(r)

    order = ("n2", "scales", "gp", "n1", "ub", "cb", "gb", "qb", "kb", "vb", "lse")
    b0 = call(
        {0: first_backward_0},
        "first_backward_0",
        loads=dict(**{n: f0[n] for n in order}, x=(tokens, 0)),
        ins=dict(grad=g0, **held),
        stores=dict(
            dh=(rows_outf, 0),
            sm=SMALLS,
            ffn=jax.ShapeDtypeStruct((FROWS, D), f32),
            att=jax.ShapeDtypeStruct((AROWS, D), f32),
        ),
        scratch=dict(total=ROWF, turned=TURNED[1], **STEP),
        aliases=dict(dh=s1.all_dh),
        vmem_mib=44, us=18,
    )

    def first_ffn_1(len_ref, r):
        ffn_back(r.grad[...].astype(f32), r, read_ends(len_ref, 1))
        r.need("start")
        ffn_terms(r, [ffn_names], r.start, r.shared(r.buffer, FCUTS))

    def second_ffn(len_ref, r):
        r.keep("all_dh", source=r.left_dh)
        ffn_terms(r, named(ffn_names), None, r.shared(r.buffer, FCUTS))

    mine = dict(**{n: f1[n] for n in order[:7]}, start=b0.ffn)
    theirs = both(("ub", "dz", "cb", "da", "gb", "df"))
    b1 = call(
        {0: (first_ffn_1, mine), 1: (second_ffn, theirs)},
        "ffn_terms",
        loads=dict(**mine, **theirs),
        ins=dict(grad=g1, left_dh=s1.dh, lines=held["lines"], w1=held["w1"], w2=held["w2"]),
        stores=dict(**streams(FCUTS), all_dh=(rows_outf, 1)),
        aliases=dict(all_dh=b0.dh),
        outs=dict(ds1=ROWF, da=ROW, sm=SMALLS),
        scratch=dict(buffer=jax.ShapeDtypeStruct((FROWS, D), bf16), total=ROWF, turned=TURNED[2], df=ROW, dz=WIDE),
        vmem_mib=44, us=8,
    )

    def first_attention_1a(len_ref, r):
        attention_back(r, read_ends(len_ref, 1), (0,))
        for n in ("dq", "dk", "dv"):
            r[n + "_0"][...] = r[n][:, 0:128]

    strip = jax.ShapeDtypeStruct((SEQ_LEN, 128), bf16)
    b2 = call(
        {0: first_attention_1a},
        "first_attention_1a",
        loads={n: f1[n] for n in order[7:]},
        through=order[7:],
        ins=dict(da=b1.da, **{n: held[n] for n in ("cos", "sin", "wo")}),
        outs=dict(dc=ROW, dq_0=strip, dk_0=strip, dv_0=strip),
        scratch=dict(dq=ROW, dk=ROW, dv=ROW),
        vmem_mib=44, us=4,
    )

    def first_attention_1b(len_ref, r):
        r.sm[...] = r.sm_in[...]
        for n in ("dq", "dk", "dv"):
            r[n][:, 0:128] = r[n + "_0"][...]
        attention_back(r, read_ends(len_ref, 1), (1, 2))
        r.need("start")
        attention_terms(r, [att_names], ("sm", "sm_0"), r.start, r.shared(r.buffer, ACUTS))
        input_back(r)

    def second_attention(len_ref, r):
        attention_terms(r, named(att_names), ("sm0", "sm1"), None, r.shared(r.buffer, ACUTS))

    early, late = Summing(FCUTS), Summing(ACUTS, 0)
    last = early.bits - 2
    early.begin([b1.kept0, b1.kept1], [b1.away0, b1.away1])
    b2, early.parts = after((dict(b2), early.parts), b2.dc)
    mine = dict(x=(tokens, 1), start=b0.att, sm_0=b0.sm)
    theirs = both(("dv", "dq", "sm", "dk"))
    b3 = call(
        {0: (first_attention_1b, mine), 1: (second_attention, theirs)},
        "attention_terms",
        loads=dict(**mine, **theirs),
        ins=dict(
            ds1=b1.ds1, sm_in=b1.sm, x0=x0, x1=x1, **b2, **{n: held[n] for n in ("cos", "sin", "wq", "wk", "wv")}
        ),
        stores=dict(dh=(rows_outf, 1), **streams(ACUTS)),
        scratch=dict(buffer=jax.ShapeDtypeStruct((AROWS, D), bf16), dq=ROW, dk=ROW, dv=ROW, sm=SMALLS),
        aliases=dict(dh=b1.all_dh),
        vmem_mib=44, us=10,
    )
    early.reduce(0)
    kept, away, *early.parts = after((b3.kept0, b3.away0, *early.parts))
    late.begin([kept], [away])

    def together():
        count = len(early.parts)
        parts = after((*early.parts, *late.parts))
        early.parts, late.parts = list(parts[:count]), list(parts[count:])

    for step in range(1, last):
        early.reduce(step, late.parts)
    together()
    def chase():
        for step in range(last - 1):
            late.reduce(step)
        return late.parts

    early.swap(chase)
    for step in range(max(0, last - 1), last):
        late.reduce(step)
    late.swap()
    for step in reversed(range(1, last)):
        early.gather(step)
    late.gather_rest(last - 1)
    early.gather(0)
    ends = early.end()
    late_ends = late.end()
    inner, outer, wo = put_together("ffn_gradients", write_ffn, core, ends, FFN_SHAPES)
    late_ends = after(late_ends, wo)
    (wq, wk, wv, bq, bk, bv, bo, g1_, s1_, c1, c2, g2, s2) = put_together(
        "attention_gradients", write_attention, core, late_ends, ATT_SHAPES
    )
    return (
        s1.rows[None],
        b3.dh[None],
        wq,
        bq,
        wk,
        bk,
        wv,
        bv,
        wo,
        bo,
        g1_,
        s1_,
        inner,
        c1,
        outer,
        c2,
        g2,
        s2,
    )


def solution(mesh):
    square, line = P("section", None, None), P("section", None)
    weights = (square, line) * 4 + (line, line) + (square, line) * 2 + (line, line)
    rows = P("section", "dp", None)
    return jax.shard_map(
        local,
        mesh=mesh,
        in_specs=(P("dp", None),) * 3 + weights,
        out_specs=(rows, rows) + weights,
        check_vma=False,
    )
```

```python
import functools
import itertools
import math

import jax
import jax.numpy as jnp
import numpy as np
from jax import lax
from jax.experimental import pallas as pl
from jax.experimental.pallas import tpu as pltpu
from jax.sharding import PartitionSpec as P

D = 384
HEADS = 6
HEAD_DIM = 64
FF = 1536
SEQ_LEN = 512
MICRO = 2
COLS = FF // D

norm_eps = 1e-12
rope_base = 10000.0
far = -1e9

bf16 = jnp.bfloat16
f32 = jnp.float32

NT = (((1,), (1,)), ((), ()))
TN = (((0,), (0,)), ((), ()))

QB, KB, VB, OB, G1, S1, C1, C2, G2, S2 = 0, 1, 2, 3, 4, 5, 6, 10, 11, 12
SMALL = 16
W1, OA, W2, OB2 = 0, 1536, 1728, 3264
FROWS, FCUTS = 3456, (896, 1728)
AQ, VA, ASMALL, AK, VB2 = 0, 384, 576, 640, 1024
AROWS, ACUTS = 1280, (640,)


def rotary_constants():
    places = np.arange(SEQ_LEN, dtype=np.float64)[:, None]
    pairs = (np.arange(128) // 2) % (HEAD_DIM // 2)
    angles = places * np.exp(pairs * (-2.0 * math.log(rope_base) / HEAD_DIM))[None, :]
    sign = np.where(np.arange(128) % 2 == 0, -1.0, 1.0)[None, :]
    return np.cos(angles).astype(np.float32), (np.sin(angles) * sign).astype(np.float32)


def dot(a, b):
    return jnp.dot(a, b, preferred_element_type=f32)


def dot_nt(a, b):
    return lax.dot_general(a, b, NT, preferred_element_type=f32)


def dot_tn(a, b):
    return lax.dot_general(a, b, TN, preferred_element_type=f32)


def segments(ends, places):
    return sum((places >= e).astype(jnp.int32) for e in ends)


def lane_iota(width=128):
    return lax.broadcasted_iota(jnp.int32, (SEQ_LEN, width), 1)


def turn(values, cos, sin):
    lane = lane_iota()
    parts = []
    for j in range(D // 128):
        u = values[:, j * 128 : (j + 1) * 128]
        partner = jnp.where(lane % 2 == 0, pltpu.roll(u, 127, 1), pltpu.roll(u, 1, 1))
        parts.append(u * cos + partner * sin)
    return jnp.concatenate(parts, axis=1)


def normalize(summed):
    centered = summed - jnp.mean(summed, axis=-1, keepdims=True)
    scale = lax.rsqrt(jnp.mean(centered * centered, axis=-1, keepdims=True) + norm_eps)
    return centered * scale, scale


def normalize_back(grad, normed, scale):
    return scale * (
        grad
        - jnp.mean(grad, axis=-1, keepdims=True)
        - normed * jnp.mean(grad * normed, axis=-1, keepdims=True)
    )


def marks(ends):
    lane = lane_iota() % HEAD_DIM
    rows = lax.broadcasted_iota(jnp.int32, (SEQ_LEN, 1), 0)
    own = lane == segments(ends, rows)
    query_marks = own.astype(f32).astype(bf16)
    key_marks = jnp.where(own | (lane > 4), 0.0, far).astype(bf16)
    return query_marks, key_marks


class Refs(dict):
    __getattr__ = dict.__getitem__


def read_ends(len_ref, block):
    ends, total = [], 0
    for j in range(4):
        total = total + len_ref[block, j]
        ends.append(total)
    return ends


def live_rows(ends):
    rows = lax.broadcasted_iota(jnp.int32, (SEQ_LEN, 1), 0)
    return (rows < ends[3]).astype(f32)


def lanes(index, width):
    if isinstance(index, int):
        return slice(index * width, (index + 1) * width)
    return pl.ds(pl.multiple_of(index * width, width), width)


F_COMPACT = (False, True)
B_COMPACT = (True, True)


def repeat(steps, step, compact):
    if compact:

        def body(j, carry):
            step(j)
            return carry

        lax.fori_loop(steps[0], steps[-1] + 1, body, 0)
    else:
        for j in steps:
            step(j)


def line(r, name):
    row = LINES[name]
    return r.lines[row : row + 1, :]


def forward(r, ends, h_ref, compact=False):
    r.need("x", "lines", "wq", "cos", "sin")
    x, cos, sin = r.x[...], r.cos[...], r.sin[...]
    r.qb[...] = turn(dot(x, r.wq[...]) + line(r, "bq"), cos, sin).astype(bf16)
    r.need("wk")
    r.kb[...] = turn(dot(x, r.wk[...]) + line(r, "bk"), cos, sin).astype(bf16)
    r.need("wv")
    r.vb[...] = (dot(x, r.wv[...]) + line(r, "bv")).astype(bf16)
    r.keep("qb", "kb", "vb")
    query_marks, key_marks = marks(ends)

    def attend(pair):
        lane = lane_iota()
        zero = jnp.zeros((SEQ_LEN, 128), bf16)
        one = jnp.ones((SEQ_LEN, 128), bf16)
        cols = lanes(pair, 128)
        q2, k2, v2 = r.qb[:, cols] * jnp.asarray(HEAD_DIM**-0.5, bf16), r.kb[:, cols], r.vb[:, cols]
        raised, tops, weighted = [], [], []
        for side in range(2):
            mine = (lane >= HEAD_DIM) == (side == 1)
            scores = dot_nt(jnp.where(mine, q2, query_marks), jnp.where(mine, k2, key_marks))
            top = jnp.max(scores, axis=-1, keepdims=True)
            raised.append(jnp.exp(scores - top).astype(bf16))
            tops.append(top)
            weighted.append(jnp.concatenate([jnp.where(mine, v2, zero), jnp.where(mine, one, zero)], axis=1))
        both = dot(jnp.concatenate(raised, axis=1), jnp.concatenate(weighted, axis=0))
        total = both[:, 128:]
        r.cb[:, cols] = (both[:, :128] / total).astype(bf16)
        log_total = jnp.log(total)
        for side in range(2):
            value = tops[side] + log_total[:, side * HEAD_DIM : side * HEAD_DIM + 1]
            r.stats[...] = jnp.where(lane == 2 * pair + side, value, r.stats[...])

    repeat(range(HEADS // 2), attend, compact)
    r.lse[...] = r.stats[...].T[:8]
    r.keep("cb", "lse")
    r.need("wo")
    attended = dot(r.cb[...], r.wo[...]) + line(r, "bo")
    n1, r1 = normalize(x.astype(f32) + attended)
    r.n1[...] = n1
    u1 = n1 * line(r, "g1") + line(r, "s1")
    r.ub[...] = u1.astype(bf16)
    r.keep("n1", "ub")
    r.total[...] = u1 + line(r, "c2")
    r.need("w1", "w2")

    def widened(j):
        cols = lanes(j, D)
        return dot(r.ub[...], r.w1[:, cols]) + r.lines[pl.ds(LINES["c1"] + j, 1), :]

    def widen(j, z):
        cols = lanes(j, D)
        below = 0.5 + 0.5 * lax.erf(z * 0.7071067811865476)
        gb = (z * below).astype(bf16)
        r.gb[:, cols] = gb
        r.gp[:, cols] = (below + z * (jnp.exp(-0.5 * z * z) * 0.3989422804014327)).astype(bf16)
        if not compact:
            r.keep("gb", "gp", cols=cols)
        r.total[...] += dot(gb, r.w2[lanes(j, D), :])

    if compact:
        repeat(range(COLS), lambda j: widen(j, widened(j)), True)
        r.keep("gb", "gp")
    else:
        z = widened(0)
        for j in range(COLS):
            following = widened(j + 1) if j + 1 < COLS else None
            widen(j, z)
            z = following
    n2, r2 = normalize(r.total[...])
    r.n2[...] = n2
    lane = lane_iota()
    r.scales[...] = jnp.where(lane == 0, r1, r2)
    h_ref[...] = ((n2 * line(r, "g2") + line(r, "s2")) * live_rows(ends)).astype(bf16)
    r.keep("n2", "scales")


def column_sum(values):
    return jnp.sum(values, axis=0, keepdims=True)


def ffn_back(grad, r, ends, compact=False):
    grad = grad * live_rows(ends)
    r.need("n2", "scales", "lines")
    n2 = r.n2[...]
    r.sm[G2 : G2 + 1, :] = column_sum(grad * n2)
    r.sm[S2 : S2 + 1, :] = column_sum(grad)
    ds2 = normalize_back(grad * line(r, "g2"), n2, r.scales[:, 1:2])
    df = ds2.astype(bf16)
    r.df[...] = df
    r.sm[C2 : C2 + 1, :] = column_sum(df.astype(f32))
    r.total[...] = ds2
    r.keep("df")
    r.need("w1", "w2", "gp")

    def widened(j):
        return dot_nt(r.df[...], r.w2[lanes(j, D), :])

    def narrow(j, wide):
        cols = lanes(j, D)
        dz = (wide * r.gp[:, cols].astype(f32)).astype(bf16)
        r.dz[:, cols] = dz
        if not compact:
            r.keep("dz", cols=cols)
        r.sm[pl.ds(C1 + j, 1), :] = column_sum(dz.astype(f32))
        r.total[...] += dot_nt(dz, r.w1[:, cols])

    if compact:
        repeat(range(COLS), lambda j: narrow(j, widened(j)), True)
        r.keep("dz")
    else:
        wide = widened(0)
        for j in range(COLS):
            following = widened(j + 1) if j + 1 < COLS else None
            narrow(j, wide)
            wide = following
    r.need("n1")
    du1, n1 = r.total[...], r.n1[...]
    r.sm[G1 : G1 + 1, :] = column_sum(du1 * n1)
    r.sm[S1 : S1 + 1, :] = column_sum(du1)
    ds1 = normalize_back(du1 * line(r, "g1"), n1, r.scales[:, 0:1])
    r.ds1[...] = ds1
    da = ds1.astype(bf16)
    r.da[...] = da
    r.sm[OB : OB + 1, :] = column_sum(da.astype(f32))
    r.keep("da", "ds1")


def attention_back(r, ends, pairs=(0, 1, 2), compact=False):
    if 0 in pairs:
        r.need("da", "wo")
        r.dc[...] = dot_nt(r.da[...], r.wo[...]).astype(bf16)
    query_marks, key_marks = marks(ends)
    r.need("qb", "kb", "vb", "lse", "cos", "sin")

    def attend(pair):
        lane = lane_iota()
        first = lane < HEAD_DIM
        zero = jnp.zeros((SEQ_LEN, 128), bf16)
        scale = jnp.asarray(HEAD_DIM**-0.5, bf16)
        cos, sin = r.cos[...], r.sin[...]
        cols = lanes(pair, 128)
        q2, k2, v2, dc2 = r.qb[:, cols] * scale, r.kb[:, cols], r.vb[:, cols], r.dc[:, cols]
        grads, dks, dvs = [], [], []
        for side in range(2):
            head = 2 * pair + side
            mine = (lane >= HEAD_DIM) == (side == 1)
            scores = dot_nt(jnp.where(mine, k2, key_marks), jnp.where(mine, q2, query_marks))
            shares = jnp.exp(scores - r.lse[pl.ds(head, 1), :])
            grad_shares = dot_nt(jnp.where(mine, v2, zero), dc2)
            row = jnp.sum(shares * grad_shares, axis=0, keepdims=True)
            grad_scores = (shares * (grad_shares - row)).astype(bf16)
            grads.append(grad_scores)
            dvs.append(dot(shares.astype(bf16), dc2))
            dks.append(dot(grad_scores, q2))
        k2s = k2 * scale
        keys = jnp.concatenate([jnp.where(first, k2s, zero), jnp.where(first, zero, k2s)], axis=0)
        dq = dot(keys.T, jnp.concatenate(grads, axis=0)).T
        dk = jnp.where(first, dks[0], dks[1])

        def back(u):
            partner = jnp.where(lane % 2 == 0, pltpu.roll(u, 127, 1), pltpu.roll(u, 1, 1))
            return (u * cos - partner * sin).astype(bf16)

        r.dq[:, cols] = back(dq)
        r.dk[:, cols] = back(dk)
        r.dv[:, cols] = jnp.where(first, dvs[0], dvs[1]).astype(bf16)
        if not compact:
            r.keep("dq", "dk", "dv", cols=cols)

    repeat(pairs, attend, compact)
    if HEADS // 2 - 1 not in pairs:
        return
    if compact:
        r.keep("dq", "dk", "dv")
    dq, dk, dv = r.dq[...], r.dk[...], r.dv[...]
    r.sm[QB : QB + 1, :] = column_sum(dq.astype(f32))
    r.sm[KB : KB + 1, :] = column_sum(dk.astype(f32))
    r.sm[VB : VB + 1, :] = column_sum(dv.astype(f32))


def input_back(r):
    r.need("ds1", "wq", "wk", "wv")
    for rows in (pl.ds(0, SEQ_LEN // 2), pl.ds(SEQ_LEN // 2, SEQ_LEN // 2)):
        dh = r.ds1[rows, :]
        for grad, weight in ((r.dq, r.wq), (r.dk, r.wk), (r.dv, r.wv)):
            dh = dh + dot_nt(grad[rows, :], weight[...])
        r.dh[rows, :] = dh
        r.keep("dh", rows=rows)
        if "dhb" in r:
            r.dhb[rows, :] = dh.astype(bf16)


def add_up(total, start, put, *places):
    for row, first, last in places:
        value = total[first:last]
        if start is not None:
            value = value + start[row : row + last - first, :].astype(f32)
        put(row, value)


def into(ref):
    def put(row, value):
        ref[row : row + value.shape[0], :] = value.astype(ref.dtype)

    return put


def ffn_terms(r, sets, start, put):
    for k, (ub, dz, gb, df, cb, da) in enumerate(sets):
        r.need(ub, dz, cb, da)
        r.turned[k] = r[ub][...].T
    total = sum(dot_tn(r[s[4]][...], r[s[5]][...]) for s in sets)
    add_up(total, start, put, (OA, 0, D // 2), (OB2, D // 2, D))
    for j in range(COLS):
        cols = lanes(j, D)
        total = sum(dot(r.turned[k], r[s[1]][:, cols]) for k, s in enumerate(sets))
        add_up(total, start, put, (W1 + j * D, 0, D))
    for s in sets:
        r.need(s[2], s[3])
    for j in range(COLS):
        cols = lanes(j, D)
        total = sum(dot_tn(r[s[2]][:, cols], r[s[3]][...]) for s in sets)
        add_up(total, start, put, (W2 + j * D, 0, D))


def attention_terms(r, sets, smalls, start, put):
    for names in sets:
        r.need(*names)

    def total(right):
        return sum(dot_tn(r[s[0]][...], r[s[right]][...]) for s in sets)

    add_up(total(3), start, put, (VA, 0, D // 2), (VB2, D // 2, D))
    add_up(total(1), start, put, (AQ, 0, D))
    if smalls:
        r.need(*smalls)
        values = sum(r[n][...] for n in smalls)
        rest = jnp.zeros((AK - ASMALL - SMALL, D), f32)
        put(ASMALL, jnp.concatenate([values, rest]))
        put(VB2 + D // 2, jnp.zeros((AROWS - VB2 - D // 2, D), f32))
    add_up(total(2), start, put, (AK, 0, D))


WNAMES = ("wq", "bq", "wk", "bk", "wv", "bv", "wo", "bo", "g1", "s1", "w1", "c1", "w2", "c2", "g2", "s2")
LINES = dict(bq=0, bk=1, bv=2, bo=3, g1=4, s1=5, c1=6, c2=10, g2=11, s2=12)
ROW = jax.ShapeDtypeStruct((SEQ_LEN, D), bf16)
ROWF = jax.ShapeDtypeStruct((SEQ_LEN, D), f32)
WIDE = jax.ShapeDtypeStruct((SEQ_LEN, FF), bf16)
LSE = jax.ShapeDtypeStruct((8, SEQ_LEN), f32)
SCALES = jax.ShapeDtypeStruct((SEQ_LEN, 128), f32)
STATE = dict(qb=ROW, kb=ROW, vb=ROW, cb=ROW, lse=LSE, n1=ROWF, ub=ROW, gb=WIDE, gp=WIDE, n2=ROWF, scales=SCALES)
STEP = dict(df=ROW, dz=WIDE, ds1=ROWF, da=ROW, dc=ROW, dq=ROW, dk=ROW, dv=ROW)
SMALLS = jax.ShapeDtypeStruct((SMALL, D), f32)
TURNED = {n: jax.ShapeDtypeStruct((n, D, SEQ_LEN), bf16) for n in (1, 2)}


def kernel_call(
    bodies, name, section, core, lengths, loads=None, ins=None, fetched=None, vectors=None, through=(), stores=None, outs=None, scratch=None,
    aliases=None, vmem_mib=44, us=5
):
    loads, ins, stores, outs, scratch = (dict(d or {}) for d in (loads, ins, stores, outs, scratch))
    fetched, vectors, aliases = fetched or {}, vectors or {}, aliases or {}
    loads = {n: a if isinstance(a, tuple) else (a, None) for n, a in loads.items()}
    stores = {n: a if isinstance(a, tuple) else (a, None) for n, a in stores.items()}
    outs.update({n: jax.ShapeDtypeStruct(a.shape, a.dtype) for n, a in fetched.items()})
    if vectors:
        outs["lines"] = SMALLS
    outs.update({n: jax.ShapeDtypeStruct(loads[n][0].shape, loads[n][0].dtype) for n in through})

    unplaced = ("kept0", "away0", "kept1", "away1", "rows", "all_dh")

    def place(shape, block):
        return pltpu.VMEM((SEQ_LEN,) + shape.shape[1:] if block is not None else shape.shape, shape.dtype)

    def part(ref, block):
        return ref if block is None else ref.at[pl.ds(block * SEQ_LEN, SEQ_LEN)]

    hbm = pl.BlockSpec(memory_space=pltpu.HBM)
    vmem = pl.BlockSpec(memory_space=pltpu.VMEM)
    smem = pl.BlockSpec(memory_space=pltpu.SMEM)
    in_names = list(ins) + list(loads) + list(vectors) + list(fetched)
    out_names = list(stores) + list(outs)
    places = {n: place(a, b) for n, (a, b) in loads.items() if n not in through}
    places.update({n: place(a, b) for n, (a, b) in stores.items() if n not in (*places, *unplaced)})
    places.update({n: pltpu.VMEM(a.shape, a.dtype) for n, a in scratch.items()})
    places.update({n: pltpu.VMEM(a.shape, a.dtype) for n, a in vectors.items()})

    def kernel(sec_ref, core_ref, len_ref, *refs):
        given = dict(zip(in_names, refs))
        rest = refs[len(in_names) + len(aliases) :]
        results = dict(zip(out_names, rest))
        own = dict(zip(places, rest[len(out_names) :]))
        sems = refs[-1]
        r = Refs(own)
        for n in ins:
            r[n] = given[n]
        for n in outs:
            r[n] = results[n]
        used = itertools.count()
        waiting = {}

        def begin(source, target):
            copy = pltpu.make_async_copy(source, target, sems.at[next(used)])
            copy.start()
            return copy

        short = [begin(given[n], own[n]) for n in vectors]
        for n in fetched:
            waiting[n] = begin(given[n], results[n])
        everywhere = list(waiting.values())

        def write_lines():
            for n, copy in zip(vectors, short):
                copy.wait()
                for j in range(vectors[n].shape[1] // D):
                    r.lines[LINES[n] + j : LINES[n] + j + 1, :] = own[n][:, j * D : (j + 1) * D].astype(f32)

        def run(body, names):
            for n in names:
                waiting[n] = begin(part(given[n], loads[n][1]), r[n])
            write_lines()
            sent = []

            def need(*names):
                for n in names:
                    if n in waiting:
                        waiting.pop(n).wait()

            def keep(*names, cols=None, rows=None, source=None):
                for n in names:
                    if n in stores:
                        target, local = part(results[n], stores[n][1]), own[n] if source is None else source
                        if cols is not None:
                            target, local = target.at[:, cols], local.at[:, cols]
                        if rows is not None:
                            target, local = target.at[rows], local.at[rows] if source is None else local
                        sent.append(begin(local, target))

            def shared(buffer, cuts):
                def put(row, value):
                    buffer[row : row + value.shape[0], :] = value.astype(buffer.dtype)
                    half = row // cuts[-1]
                    for k, (low, high) in enumerate(zip((0, *cuts), cuts)):
                        first = max(row, half * cuts[-1] + low)
                        last = min(row + value.shape[0], half * cuts[-1] + high)
                        if first >= last:
                            continue
                        target, sem = pl.ds(first - half * cuts[-1] - low, last - first), sems.at[next(used)]
                        copies = [
                            pltpu.make_async_copy(buffer.at[pl.ds(first, last - first)], results[f"{n}{k}"].at[target], sem)
                            for n in ("kept", "away")
                        ]
                        pl.when(core_ref[0] == half)(copies[0].start)
                        pl.when(core_ref[0] != half)(copies[1].start)
                        sent.append(copies[0])

                return put

            r.update(need=need, keep=keep, shared=shared)
            body(len_ref, r)
            need(*list(waiting))
            for copy in sent:
                copy.wait()

        def idle():
            write_lines()
            for copy in everywhere:
                copy.wait()

        for k in range(2):
            if k in bodies:
                body, names = bodies[k] if isinstance(bodies[k], tuple) else (bodies[k], loads)
                pl.when(sec_ref[0] == k)(functools.partial(run, body, names))
            elif fetched:
                pl.when(sec_ref[0] == k)(idle)

    def pinned(array):
        return pltpu.with_memory_space_constraint(array, pltpu.HBM)

    results = pl.pallas_call(
        kernel,
        out_shape=[pltpu.HBM(a.shape, a.dtype) for a, _ in stores.values()] + list(outs.values()),
        in_specs=[smem] * 3 + [vmem] * len(ins) + [hbm] * (len(loads) + len(vectors) + len(fetched) + len(aliases)),
        out_specs=[hbm] * len(stores) + [vmem] * len(outs),
        scratch_shapes=list(places.values()) + [pltpu.SemaphoreType.DMA((64,))],
        input_output_aliases={3 + len(in_names) + k: out_names.index(n) for k, n in enumerate(aliases)},
        compiler_params=pltpu.CompilerParams(vmem_limit_bytes=vmem_mib * 1024 * 1024),
        cost_estimate=pl.CostEstimate(flops=int(us * 1.15e9), bytes_accessed=0, transcendentals=0),
        name=name,
    )(
        section,
        core,
        lengths,
        *ins.values(),
        *[pinned(a) for a, _ in loads.values()],
        *[pinned(a) for a in vectors.values()],
        *[pinned(a) for a in fetched.values()],
        *[pinned(a) for a in aliases.values()],
    )
    return Refs(zip(out_names, results))


def flipped(block, mask):
    return lax.ppermute(block, "dp", [(i, i ^ mask) for i in range(lax.axis_size("dp"))])


def exchange(block, axis, bit):
    return flipped(block, 1 << bit)


def shifted(block, axis, distance):
    devices = range(lax.axis_size(axis))
    route = [(i - distance, i) for i in devices if i - distance in devices]
    return lax.ppermute(block, axis, route)


def reduce_step(block, bit, index, others=()):
    half = block.shape[0] // 2
    side = (index >> bit) & 1
    away = lax.dynamic_slice_in_dim(block, (1 - side) * half, half, 0)
    kept = lax.dynamic_slice_in_dim(block, side * half, half, 0)
    received = exchange(away, "dp", bit)
    if others:
        kept = after((kept,), *others)[0]
    return (kept.astype(f32) + received.astype(f32)).astype(bf16)


def gather_step(block, bit, index):
    side = (index >> bit) & 1
    other = exchange(block, "dp", bit)
    return jnp.where(side == 0, jnp.concatenate([block, other]), jnp.concatenate([other, block]))


def gather_two(block, low_bit, high_bit, index):
    both = flipped(block, (1 << low_bit) | (1 << high_bit))
    high = flipped(block, 1 << high_bit)
    low = flipped(block, 1 << low_bit)
    at_low, at_high = (index >> low_bit) & 1 == 0, (index >> high_bit) & 1 == 0

    def order(first, second, straight):
        return jnp.where(straight, jnp.concatenate([first, second]), jnp.concatenate([second, first]))

    return order(order(block, low, at_low), order(high, both, at_low), at_high)


class Summing:
    def __init__(self, cuts, turned=1):
        self.cuts = cuts
        self.index = lax.axis_index("dp")
        self.bits = lax.axis_size("dp").bit_length() - 1
        self.orders = [list(range(1, self.bits)) for _ in cuts]
        if self.bits > 2:
            for order in self.orders[turned:]:
                order[0], order[1] = order[1], order[0]

    def begin(self, kept, away):
        self.parts = [
            (mine.astype(f32) + exchange(other, "dp", 0).astype(f32)).astype(bf16) for mine, other in zip(kept, away)
        ]

    def reduce(self, step, others=()):
        self.parts = [reduce_step(p, o[step], self.index, others) for p, o in zip(self.parts, self.orders)]

    def gather(self, step):
        self.parts = [gather_step(p, o[step], self.index) for p, o in zip(self.parts, self.orders)]

    def swap(self, meanwhile=lambda: ()):
        others = [exchange(p, "dp", o[-1]) for p, o in zip(self.parts, self.orders)]
        parts = after(self.parts, *meanwhile())
        self.parts = [(p.astype(f32) + q.astype(f32)).astype(bf16) for p, q in zip(parts, others)]

    def gather_rest(self, step):
        while step > 1:
            self.gather(step)
            step -= 1
        self.parts = [
            gather_two(p, o[1], o[0], self.index) if step == 1 else p for p, o in zip(self.parts, self.orders)
        ]
        if step == 0:
            self.gather(0)

    def wait(self, *others):
        self.parts = list(after(self.parts, *others))

    def end(self):
        return self.parts, [exchange(part, "dp", 0) for part in self.parts]


def after(arrays, *others):
    return lax.optimization_barrier((tuple(arrays), others))[0]


def put_together(name, write, core, halves, shapes):
    mine, other = halves
    bounds = [0]
    for part in mine:
        bounds.append(bounds[-1] + part.shape[0])
    count = len(mine)
    large = [k for k, shape in enumerate(shapes) if len(shape) == 3]

    def kernel(core_ref, *refs):
        own, away, results = refs[:count], refs[count : 2 * count], refs[2 * count : 2 * count + len(shapes)]
        outs, sems = list(results), refs[-1]
        for place, k in zip(refs[2 * count + len(shapes) :], large):
            outs[k] = place

        def rows(half):
            mine_here = core_ref[0] == half

            def get(first, last):
                pieces = []
                for k, (low, high) in enumerate(zip(bounds, bounds[1:])):
                    if first < high and last > low:
                        part = slice(max(first, low) - low, min(last, high) - low)
                        pieces.append(jnp.where(mine_here, own[k][part, :], away[k][part, :]).astype(f32))
                return pieces[0] if len(pieces) == 1 else jnp.concatenate(pieces)

            return get

        sent = []

        def send(k, part=slice(None)):
            copy = pltpu.make_async_copy(outs[k].at[:, part], results[k].at[:, part], sems.at[len(sent)])
            copy.start()
            sent.append(copy)

        write(rows(0), rows(1), outs, send)
        for copy in sent:
            copy.wait()

    vmem = pl.BlockSpec(memory_space=pltpu.VMEM)
    hbm = pl.BlockSpec(memory_space=pltpu.HBM)
    return pl.pallas_call(
        kernel,
        out_shape=[pltpu.HBM(s, f32) if k in large else jax.ShapeDtypeStruct(s, f32) for k, s in enumerate(shapes)],
        in_specs=[pl.BlockSpec(memory_space=pltpu.SMEM)] + [vmem] * (2 * count),
        out_specs=[hbm if k in large else vmem for k in range(len(shapes))],
        scratch_shapes=[pltpu.VMEM(shapes[k], f32) for k in large] + [pltpu.SemaphoreType.DMA((16,))],
        compiler_params=pltpu.CompilerParams(vmem_limit_bytes=20 * 1024 * 1024),
        name=name,
    )(core, *mine, *other)


def write_ffn(low, high, outs, send):
    inner, outer, wo = outs
    for j in range(COLS):
        rows = slice(j * D, (j + 1) * D)
        inner[0, :, rows] = low(j * D, (j + 1) * D)
        outer[0, rows, :] = high(j * D, (j + 1) * D)
        send(1, rows)
    send(0)
    wo[0, 0 : D // 2] = low(OA, W2)
    wo[0, D // 2 : D] = high(OA, W2)
    send(2)


def write_attention(low, high, outs, send):
    wq, wk, wv, bq, bk, bv, bo, g1, s1, c1, c2, g2, s2 = outs
    wq[0] = low(AQ, VA)
    wk[0] = high(AQ, VA)
    wv[0, 0 : D // 2] = low(VA, ASMALL)
    wv[0, D // 2 : D] = high(VA, ASMALL)
    for k in range(3):
        send(k)
    small = low(ASMALL, ASMALL + SMALL)
    for ref, row in ((bq, QB), (bk, KB), (bv, VB), (bo, OB), (g1, G1), (s1, S1), (c2, C2), (g2, G2), (s2, S2)):
        ref[...] = small[row : row + 1, :]
    for j in range(COLS):
        c1[:, j * D : (j + 1) * D] = small[C1 + j : C1 + j + 1, :]


FFN_SHAPES = [(1, D, FF), (1, FF, D), (1, D, D)]
ATT_SHAPES = [(1, D, D)] * 3 + [(1, D)] * 6 + [(1, FF)] + [(1, D)] * 3


def local(tokens, cotangent, lengths, *weights):
    section = lax.axis_index("section").astype(jnp.int32).reshape(1)
    core = (lax.axis_index("dp") & 1).astype(jnp.int32).reshape(1)
    cos, sin = rotary_constants()
    w = dict(zip(WNAMES, (m[0] if m.ndim == 3 else m for m in weights)))
    call = functools.partial(kernel_call, section=section, core=core, lengths=lengths)
    rows_out = jax.ShapeDtypeStruct(tokens.shape, bf16)
    rows_outf = jax.ShapeDtypeStruct(tokens.shape, f32)

    def streams(cuts):
        sizes = [high - low for low, high in zip((0, *cuts), cuts)]
        return {n + str(k): jax.ShapeDtypeStruct((m, D), bf16) for n in ("kept", "away") for k, m in enumerate(sizes)}

    held = {n: w[n] for n in ("wq", "wk", "wv", "wo", "w1", "w2")}
    held = dict(wq=held.pop("wq"), cos=jnp.asarray(cos), sin=jnp.asarray(sin), **held)

    last_state = {n: STATE[n] for n in ("n2", "scales")}

    def first_forward(block, held, fetch, left):
        def body(len_ref, r):
            for n in left:
                r.keep(n + "_0", source=r["left_" + n])
            forward(r, read_ends(len_ref, block), r.h, F_COMPACT[block])
            if not fetch:
                r.keep("rows", rows=pl.ds(0, SEQ_LEN), source=r.left_h)
                r.keep("rows", rows=pl.ds(SEQ_LEN, SEQ_LEN), source=r.h)

        return call(
            {0: body},
            f"first_forward_{block}",
            loads=dict(x=(tokens, block)),
            ins={} if fetch else dict(**held, **{"left_" + n: a for n, a in left.items()}),
            fetched=held if fetch else {},
            vectors={n: w[n] for n in LINES} if fetch else {},
            stores=dict(
                **{n: a for n, a in STATE.items() if not (fetch and n in last_state)},
                **{n + "_0": STATE[n] for n in left if n in STATE},
                **({} if fetch else dict(rows=rows_out)),
            ),
            outs=dict(h=ROW, **(last_state if fetch else {})),
            scratch=dict(stats=SCALES, total=ROWF),
            vmem_mib=44, us=10,
        )

    f0 = first_forward(0, held, True, {})
    held = {n: f0[n] for n in ("lines", *held)}
    x0 = shifted(f0.h, "section", 1)
    f1 = first_forward(1, held, False, {n: f0[n] for n in (*last_state, "h")})
    f0.update({n: f1[n + "_0"] for n in last_state})
    x1 = shifted(f1.h, "section", 1)

    kept = ("cb", "ub", "gb", "df", "dz", "da", "dq", "dk", "dv")
    every = dict(**STATE, **STEP)

    def second_layer(block, x, before, left):
        def body(len_ref, r):
            ends = read_ends(len_ref, block)
            forward(r, ends, r.h)
            r.keep("rows", source=r.h)
            r.need("cotangent")
            ffn_back(r.cotangent[...], r, ends)
            attention_back(r, ends, compact=B_COMPACT[block])
            r.keep("sm")
            input_back(r)
            if block:
                r.keep("all_dh", source=r.left_dh)

        return call(
            {1: body},
            f"second_layer_{block}",
            loads=dict(cotangent=(cotangent, block)),
            ins=dict(x=x, **held, **left),
            stores=dict(
                rows=(rows_out, block),
                sm=SMALLS,
                **{n: every[n] for n in kept},
                **(dict(all_dh=(rows_outf, 0)) if block else {}),
            ),
            outs=dict(dhb=ROW, dh=ROWF),
            scratch=dict(h=ROW, stats=SCALES, total=ROWF, **{n: every[n] for n in every if n not in kept}),
            aliases=before,
            vmem_mib=44, us=20,
        )

    s0 = second_layer(0, x0, dict(rows=f1.rows), {})
    g0 = shifted(s0.dhb, "section", -1)
    s1 = second_layer(1, x1, dict(rows=s0.rows), dict(left_dh=s0.dh))
    g1 = shifted(s1.dhb, "section", -1)

    def both(names):
        return {n + str(b): s[n] for b, s in enumerate((s0, s1)) for n in names}

    ffn_names = ("ub", "dz", "gb", "df", "cb", "da")
    att_names = ("x", "dq", "dk", "dv")

    def named(names):
        return [[n + str(b) for n in names] for b in range(MICRO)]

    def first_backward_0(len_ref, r):
        ends = read_ends(len_ref, 0)
        ffn_back(r.grad[...].astype(f32), r, ends, True)
        ffn_terms(r, [ffn_names], None, into(r.ffn))
        r.keep("ffn")
        attention_back(r, ends, compact=True)
        r.keep("sm")
        attention_terms(r, [att_names], None, None, into(r.att))
        r.keep("att")
        input_back(r)

    order = ("n2", "scales", "gp", "n1", "ub", "cb", "gb", "qb", "kb", "vb", "lse")
    b0 = call(
        {0: first_backward_0},
        "first_backward_0",
        loads=dict(**{n: f0[n] for n in order}, x=(tokens, 0)),
        ins=dict(grad=g0, **held),
        stores=dict(
            dh=(rows_outf, 0),
            sm=SMALLS,
            ffn=jax.ShapeDtypeStruct((FROWS, D), bf16),
            att=jax.ShapeDtypeStruct((AROWS, D), bf16),
        ),
        scratch=dict(total=ROWF, turned=TURNED[1], **STEP),
        aliases=dict(dh=s1.all_dh),
        vmem_mib=44, us=18,
    )

    def first_ffn_1(len_ref, r):
        ffn_back(r.grad[...].astype(f32), r, read_ends(len_ref, 1))
        r.need("start")
        ffn_terms(r, [ffn_names], r.start, r.shared(r.buffer, FCUTS))

    def second_ffn(len_ref, r):
        r.keep("all_dh", source=r.left_dh)
        ffn_terms(r, named(ffn_names), None, r.shared(r.buffer, FCUTS))

    mine = dict(**{n: f1[n] for n in order[:7]}, start=b0.ffn)
    theirs = both(("ub", "dz", "cb", "da", "gb", "df"))
    b1 = call(
        {0: (first_ffn_1, mine), 1: (second_ffn, theirs)},
        "ffn_terms",
        loads=dict(**mine, **theirs),
        ins=dict(grad=g1, left_dh=s1.dh, lines=held["lines"], w1=held["w1"], w2=held["w2"]),
        stores=dict(**streams(FCUTS), all_dh=(rows_outf, 1)),
        aliases=dict(all_dh=b0.dh),
        outs=dict(ds1=ROWF, da=ROW, sm=SMALLS),
        scratch=dict(buffer=jax.ShapeDtypeStruct((FROWS, D), bf16), total=ROWF, turned=TURNED[2], df=ROW, dz=WIDE),
        vmem_mib=44, us=8,
    )

    def first_attention_1a(len_ref, r):
        attention_back(r, read_ends(len_ref, 1), (0,))
        for n in ("dq", "dk", "dv"):
            r[n + "_0"][...] = r[n][:, 0:128]

    strip = jax.ShapeDtypeStruct((SEQ_LEN, 128), bf16)
    b2 = call(
        {0: first_attention_1a},
        "first_attention_1a",
        loads={n: f1[n] for n in order[7:]},
        through=order[7:],
        ins=dict(da=b1.da, **{n: held[n] for n in ("cos", "sin", "wo")}),
        outs=dict(dc=ROW, dq_0=strip, dk_0=strip, dv_0=strip),
        scratch=dict(dq=ROW, dk=ROW, dv=ROW),
        vmem_mib=44, us=4,
    )

    def first_attention_1b(len_ref, r):
        r.sm[...] = r.sm_in[...]
        for n in ("dq", "dk", "dv"):
            r[n][:, 0:128] = r[n + "_0"][...]
        attention_back(r, read_ends(len_ref, 1), (1, 2))
        r.need("start")
        attention_terms(r, [att_names], ("sm", "sm_0"), r.start, r.shared(r.buffer, ACUTS))
        input_back(r)

    def second_attention(len_ref, r):
        attention_terms(r, named(att_names), ("sm0", "sm1"), None, r.shared(r.buffer, ACUTS))

    early, late = Summing(FCUTS), Summing(ACUTS, 0)
    last = early.bits - 2
    early.begin([b1.kept0, b1.kept1], [b1.away0, b1.away1])
    b2, early.parts = after((dict(b2), early.parts), b2.dc)
    mine = dict(x=(tokens, 1), start=b0.att, sm_0=b0.sm)
    theirs = both(("dv", "dq", "sm", "dk"))
    b3 = call(
        {0: (first_attention_1b, mine), 1: (second_attention, theirs)},
        "attention_terms",
        loads=dict(**mine, **theirs),
        ins=dict(
            ds1=b1.ds1, sm_in=b1.sm, x0=x0, x1=x1, **b2, **{n: held[n] for n in ("cos", "sin", "wq", "wk", "wv")}
        ),
        stores=dict(dh=(rows_outf, 1), **streams(ACUTS)),
        scratch=dict(buffer=jax.ShapeDtypeStruct((AROWS, D), bf16), dq=ROW, dk=ROW, dv=ROW, sm=SMALLS),
        aliases=dict(dh=b1.all_dh),
        vmem_mib=44, us=10,
    )
    early.reduce(0)
    kept, away, *early.parts = after((b3.kept0, b3.away0, *early.parts))
    late.begin([kept], [away])

    def together():
        count = len(early.parts)
        parts = after((*early.parts, *late.parts))
        early.parts, late.parts = list(parts[:count]), list(parts[count:])

    for step in range(1, last):
        early.reduce(step, late.parts)
    together()
    def chase():
        for step in range(last - 1):
            late.reduce(step)
        return late.parts

    early.swap(chase)
    for step in range(max(0, last - 1), last):
        late.reduce(step)
    late.swap()
    for step in reversed(range(1, last)):
        early.gather(step)
    late.gather_rest(last - 1)
    early.gather(0)
    ends = early.end()
    late_ends = late.end()
    inner, outer, wo = put_together("ffn_gradients", write_ffn, core, ends, FFN_SHAPES)
    late_ends = after(late_ends, wo)
    (wq, wk, wv, bq, bk, bv, bo, g1_, s1_, c1, c2, g2, s2) = put_together(
        "attention_gradients", write_attention, core, late_ends, ATT_SHAPES
    )
    return (
        s1.rows[None],
        b3.dh[None],
        wq,
        bq,
        wk,
        bk,
        wv,
        bv,
        wo,
        bo,
        g1_,
        s1_,
        inner,
        c1,
        outer,
        c2,
        g2,
        s2,
    )


def solution(mesh):
    square, line = P("section", None, None), P("section", None)
    weights = (square, line) * 4 + (line, line) + (square, line) * 2 + (line, line)
    rows = P("section", "dp", None)
    return jax.shard_map(
        local,
        mesh=mesh,
        in_specs=(P("dp", None),) * 3 + weights,
        out_specs=(rows, rows) + weights,
        check_vma=False,
    )
```
